256 devices in a mesh: dp: 16 (over z, core), seq: 16 (over x, y).
Axes of the slice: x: 4, y: 4, z: 8, core: 2. Of those that a mesh axis runs over, the one named last changes fastest.
Arguments:
- queries: bfloat16 [32768, 2048], P(('dp', 'seq')), may hold values from -10 to 10
- keys: bfloat16 [32768, 2048], P(('dp', 'seq')), may hold values from -10 to 10
- values: bfloat16 [32768, 2048], P(('dp', 'seq')), may hold values from -6 to 6
- attn: bfloat16 [32768, 2048], P(('dp', 'seq')), may hold values from -6 to 6
- grad_out: bfloat16 [32768, 4096], P(('dp', 'seq')), may hold values from -24 to 24
- w_out: bfloat16 [2048, 4096], P('seq'), may hold values from -0.125 to 0.125
- starts: int32 [16, 8], P('dp'), may hold values from 0 to 2047, as said below
Outputs:
- grad_queries: bfloat16 [32768, 2048], P(('dp', 'seq'))
- grad_keys: bfloat16 [32768, 2048], P(('dp', 'seq'))
- grad_values: bfloat16 [32768, 2048], P(('dp', 'seq'))
- grad_w_out: float32 [2048, 4096], P('seq', 'dp')
The draws below stay inside these ranges and needn't reach their ends.
Inputs may be any that keep to these rules, and one draw needn't show every extreme that they name: starts[r, 0] = 0 and each row is strictly increasing.
All inputs are finite; a program needn't handle non-finite values.
Results may differ from the reference program's by a relative error of at most 0.022.
Values may be sent and summed in bfloat16 or wider, within the bound.
A program may use at most 128 MiB of HBM per device.

```python
import jax
import jax.numpy as jnp
from jax import lax

D = 4096
HDIM = 128
HEADS = 16
EPIS = 8
SEQLEN = 2048
TOKENS = 32768
HW = 2048
N_DP = 16


def draw_queries(key, part):
    key = jax.random.fold_in(key, 21)
    return jnp.clip(jax.random.normal(key, (TOKENS, HW), jnp.float32), -6.0, 6.0).astype(jnp.bfloat16)


def draw_keys(key, part):
    key = jax.random.fold_in(key, 33)
    return jnp.clip(jax.random.normal(key, (TOKENS, HW), jnp.float32), -6.0, 6.0).astype(jnp.bfloat16)


def draw_starts(key, part):
    key = jax.random.fold_in(key, 5)
    row_key, pick_key = jax.random.split(key)
    keys_all = jax.random.split(row_key, N_DP)

    def one_row(one_key):
        picked = jax.random.permutation(one_key, SEQLEN - 2)[:EPIS - 1].astype(jnp.int32) + 1
        return jnp.concatenate([jnp.zeros((1,), jnp.int32), jnp.sort(picked)])
    table = jax.vmap(one_row)(keys_all).astype(jnp.int32)
    target = jax.random.randint(pick_key, (), 0, N_DP).astype(jnp.int32)
    rows = jnp.arange(N_DP).astype(jnp.int32)
    cols = jnp.arange(EPIS).astype(jnp.int32)
    hit = (rows[:, None] == target) & (cols[None, :] == EPIS - 1)
    return jnp.where(hit, jnp.int32(SEQLEN - 1), table).astype(jnp.int32)


def raised(drawn, rng, source, target, shards_of, factor):
    owner, partner = [(jnp.arange(drawn.shape[position]) // (drawn.shape[position] // shards_of)).reshape([-1 if axis == position else 1 for axis in range(drawn.ndim)]) for position in (source, target)]
    chosen = jax.random.permutation(rng, shards_of)[partner]
    strong = (owner == chosen) | (owner == (partner + shards_of // 2) % shards_of)
    return jnp.where(strong, factor * drawn, drawn)


def steps_of(own_key, dims, shards, low, top_value):
    gain, own = 1.0, jax.random.fold_in(own_key, 6)
    for axis_at, parts in shards:
        draws = jnp.exp(jax.random.uniform(jax.random.fold_in(own, axis_at), (parts,), jnp.float32, low / len(shards), top_value / len(shards)))
        gain = gain * jnp.repeat(draws, dims[axis_at] // parts).reshape([-1 if axis == axis_at else 1 for axis in range(len(dims))])
    return gain


def normal_values(own_key, shape, deviation, limit, cuts=(), dtype=jnp.bfloat16):
    values = jax.random.normal(own_key, shape, jnp.float32) * deviation
    if len(cuts) > 0:
        values = steps_of(own_key, shape, cuts, -0.22, 0.18) * values
    return jnp.clip(values, min=-limit, max=limit).astype(dtype)


def heavy_noise(rng, dims, scale, reach, pieces, heavy, dtype=jnp.bfloat16):
    result = scale * jax.random.normal(rng, dims, jnp.float32)
    if pieces:
        result = result * steps_of(rng, dims, pieces, -0.22, 0.18)
    return jnp.clip(raised(result, jax.random.fold_in(rng, 3), *heavy), -reach, reach).astype(dtype)


def setup_inputs(seed: int = 0) -> dict:
    arg_keys = jax.random.split(jax.random.key(seed), 8)
    queries = draw_queries(jax.random.fold_in(arg_keys[7], 71), 0)
    keys = draw_keys(jax.random.fold_in(arg_keys[7], 71), 0)
    values = normal_values(arg_keys[2], (TOKENS, HW), 1.0, 6.0, ((0, 256),))
    attn = normal_values(arg_keys[3], (TOKENS, HW), 1.0, 6.0, ((0, 256),))
    grad_out = heavy_noise(arg_keys[4], (TOKENS, D), 1.0, 24.0, ((0, 256),), (0, 1, 256, 6.0))
    w_out = normal_values(arg_keys[5], (HW, D), HW ** -0.5, 0.125, ((0, 16),))
    starts = draw_starts(jax.random.fold_in(arg_keys[7], 71), 0)
    return {"queries": queries, "keys": keys, "values": values, "attn": attn, "grad_out": grad_out, "w_out": w_out, "starts": starts}


def head_grads(q, k, v, o, g, seg):
    scale = HDIM ** -0.5
    pos = jnp.arange(q.shape[0])
    live = (pos[None, :] <= pos[:, None]) & (pos[None, :] >= seg[:, None])
    scores = jnp.dot(q, k.T, preferred_element_type=jnp.float32) * scale
    top = jnp.max(jnp.where(live, scores, -jnp.inf), axis=-1, keepdims=True)
    prob = jnp.where(live, jnp.exp(scores - top), 0.0)
    prob = prob / jnp.sum(prob, axis=-1, keepdims=True)
    prob_b = prob.astype(jnp.bfloat16)
    grad_v = jnp.dot(prob_b.T, g, preferred_element_type=jnp.float32)
    grad_prob = jnp.dot(g, v.T, preferred_element_type=jnp.float32)
    row_dot = jnp.sum(g.astype(jnp.float32) * o.astype(jnp.float32), axis=-1, keepdims=True)
    grad_s = (prob * (grad_prob - row_dot)).astype(jnp.bfloat16)
    grad_q = scale * jnp.dot(grad_s, k, preferred_element_type=jnp.float32)
    grad_k = scale * jnp.dot(grad_s.T, q, preferred_element_type=jnp.float32)
    return grad_q.astype(jnp.bfloat16), grad_k.astype(jnp.bfloat16), grad_v.astype(jnp.bfloat16)


def reference(queries, keys, values, attn, grad_out, w_out, starts):
    grad_attn = jnp.dot(grad_out, w_out.T, preferred_element_type=jnp.float32).astype(jnp.bfloat16)
    grad_w_out = jnp.dot(attn.T, grad_out, preferred_element_type=jnp.float32)
    pos = jnp.arange(SEQLEN)
    seg_all = jnp.max(jnp.where(starts[:, None, :] <= pos[None, :, None], starts[:, None, :], 0), axis=-1)

    def split_heads(a):
        return a.reshape(N_DP, SEQLEN, HEADS, HDIM).transpose(0, 2, 1, 3)

    def one_replica(items):
        q, k, v, o, g, seg = items
        return lax.map(lambda h: head_grads(h[0], h[1], h[2], h[3], h[4], seg), (q, k, v, o, g))

    grad_q, grad_k, grad_v = lax.map(one_replica, (split_heads(queries), split_heads(keys), split_heads(values), split_heads(attn), split_heads(grad_attn), seg_all))

    def join_heads(a):
        return a.transpose(0, 2, 1, 3).reshape(TOKENS, HW)

    return join_heads(grad_q), join_heads(grad_k), join_heads(grad_v), grad_w_out
```

```python
import functools

import jax
import jax.numpy as jnp
from jax import lax
from jax.experimental import pallas as pl
from jax.experimental.pallas import tpu as pltpu
from jax.sharding import PartitionSpec as P

HDIM = 128
MESH = pl.DeviceIdType.MESH
BF16 = jnp.bfloat16
F32 = jnp.float32
NT = (((1,), (1,)), ((), ()))
NN = (((1,), (0,)), ((), ()))
TN = (((0,), (0,)), ((), ()))
VMEM_LIMIT = 56 << 20


def place():
    dp = lax.axis_index("dp")
    s = lax.axis_index("seq")
    c = dp % 2
    x, y = s // 4, s % 4
    p = x * (1 - c) + y * c
    q = y * (1 - c) + x * c
    sp, sq = 4 - 3 * c, 1 + 3 * c

    def block(pp, qq):
        return pp * sp + qq * sq

    return dp, c, s, p, q, block


def remote(src, dst, ssem, rsem, dp, s):
    cp = pltpu.make_async_remote_copy(
        src_ref=src, dst_ref=dst, send_sem=ssem, recv_sem=rsem, device_id=(dp, s), device_id_type=MESH
    )
    cp.start()


def drain(ref, sem):
    pltpu.make_async_copy(ref, ref, sem).wait()


def rows(i, n=128):
    return pl.ds(pl.multiple_of(i * n, n), n)


def gather_kernel(
    q_in, k_in, v_in, o_in, g_in, w_in,
    qh, kh, vh, gh, rdh, dwp,
    gbuf, wbuf, abuf, atbuf, gsnd, rdsnd, dwv,
    g_rs, w_rs, a_rs, h_rs, ga_rs, rd_rs,
    g_ss, w_ss, a_ss, h_ss, ga_ss, rd_ss, loc, dw_sem,
):
    dp, c, s, p, q, block = place()
    bar = pltpu.get_barrier_semaphore()
    for a in range(4):
        for b in range(4):
            if a or b:
                pl.semaphore_signal(
                    bar, 1, device_id=(dp, block((p + a) % 4, (q + b) % 4)), device_id_type=MESH
                )

    lg = pltpu.make_async_copy(g_in, gbuf.at[rows(q)], loc.at[0])
    lw = pltpu.make_async_copy(w_in, wbuf.at[rows(p)], loc.at[1])
    lg.start()
    lw.start()
    la = []
    for pp in range(4):
        cp = pltpu.make_async_copy(
            o_in.at[:, rows(block(pp, q))], abuf.at[rows(q), pl.ds(pp * 128, 128)], loc.at[2 + pp]
        )
        cp.start()
        la.append(cp)
    lh = []
    for t, (src, dst) in enumerate(((q_in, qh), (k_in, kh), (v_in, vh))):
        cp = pltpu.make_async_copy(src.at[:, rows(s)], dst.at[rows(s)], loc.at[6 + t])
        cp.start()
        lh.append(cp)

    pl.semaphore_wait(bar, 15)
    for b in (1, 3, 2):
        qq = (q + b) % 4
        remote(g_in, gbuf.at[rows(q)], g_ss, g_rs.at[q], dp, block(p, qq))
        pp = (p + b) % 4
        remote(w_in, wbuf.at[rows(p)], w_ss, w_rs.at[p], dp, block(pp, q))
        for f in range(4):
            remote(
                o_in.at[:, rows(block(f, qq))], abuf.at[rows(q), pl.ds(f * 128, 128)], a_ss, a_rs, dp, block(p, qq)
            )

    lg.wait()
    lw.wait()
    for cp in la:
        cp.wait()
    for b in (1, 3, 2):
        qq = (q + b) % 4
        drain(gbuf.at[rows(qq)], g_rs.at[qq])
        pp = (p + b) % 4
        drain(wbuf.at[rows(pp)], w_rs.at[pp])
    drain(abuf.at[pl.ds(0, 384)], a_rs)

    for a in range(4):
        for b in range(4):
            if a or b:
                d = block((p + a) % 4, (q + b) % 4)
                for t, (src, dst) in enumerate(((q_in, qh), (k_in, kh), (v_in, vh))):
                    remote(src.at[:, rows(d)], dst.at[rows(s)], h_ss.at[t], h_rs.at[t], dp, d)

    ones = jnp.ones((8, 128), F32)
    for n in range(2):
        ga = lax.dot_general(
            gbuf[...], wbuf[pl.ds(n * 256, 256), :], NT, preferred_element_type=F32
        ).astype(BF16)
        for m in range(2):
            f = n * 2 + m
            gf = ga[:, m * 128 : (m + 1) * 128]
            gsnd[f] = gf
            prod = gf.astype(F32) * abuf[:, f * 128 : (f + 1) * 128].astype(F32)
            rd = lax.dot_general(ones, prod, NT, preferred_element_type=F32, precision=lax.Precision.HIGHEST)
            for t in range(4):
                rdsnd[f, t] = rd[:, t * 128 : (t + 1) * 128]

    lga = []
    for b in range(4):
        cp = pltpu.make_async_copy(gsnd.at[p, pl.ds(b * 128, 128)], gh.at[rows(block(p, b))], loc.at[9 + b])
        cp.start()
        lga.append(cp)
        cp = pltpu.make_async_copy(rdsnd.at[p, b], rdh.at[block(p, b)], loc.at[13 + b])
        cp.start()
        lga.append(cp)
    for a in (1, 3, 2):
        pp = (p + a) % 4
        for b in range(4):
            remote(gsnd.at[pp, pl.ds(b * 128, 128)], gh.at[rows(block(p, b))], ga_ss, ga_rs, dp, block(pp, q))
            remote(rdsnd.at[pp, b], rdh.at[block(p, b)], rd_ss, rd_rs, dp, block(pp, q))

    atbuf[...] = abuf[...].T

    @pl.loop(0, 8)
    def _(n):
        cols = rows(n, 512)
        dwv[:, cols] = lax.dot_general(
            atbuf[...], gbuf[:, cols], NN, preferred_element_type=F32
        ).astype(BF16)

    cdw = pltpu.make_async_copy(dwv, dwp, dw_sem)
    cdw.start()

    for cp in lga:
        cp.wait()
    for cp in lh:
        cp.wait()
    drain(gsnd.at[pl.ds(0, 3)], ga_rs)
    drain(rdsnd.at[pl.ds(0, 3)], rd_rs)
    for t, dst in enumerate((qh, kh, vh)):
        drain(dst.at[pl.ds(0, 1920)], h_rs.at[t])
    cdw.wait()
    drain(gbuf.at[pl.ds(0, 384)], g_ss)
    drain(wbuf.at[pl.ds(0, 384)], w_ss)
    drain(abuf.at[pl.ds(0, 384)], a_ss)
    drain(gsnd.at[pl.ds(0, 3)], ga_ss)
    drain(rdsnd.at[pl.ds(0, 3)], rd_ss)
    for t, dst in enumerate((qh, kh, vh)):
        drain(dst.at[pl.ds(0, 1920)], h_ss.at[t])


def gather(queries, keys, values, attn, grad_out, w_out):
    any_ = pl.BlockSpec(memory_space=pl.ANY)
    head = jax.ShapeDtypeStruct((2048, 128), BF16)
    dma = pltpu.SemaphoreType.DMA
    return pl.pallas_call(
        gather_kernel,
        out_shape=(head, head, head, head, jax.ShapeDtypeStruct((16, 8, 128), F32),
                   jax.ShapeDtypeStruct((512, 4096), BF16)),
        in_specs=[any_] * 6,
        out_specs=(any_,) * 6,
        scratch_shapes=[
            pltpu.VMEM((512, 4096), BF16), pltpu.VMEM((512, 4096), BF16), pltpu.VMEM((512, 512), BF16),
            pltpu.VMEM((512, 512), BF16), pltpu.VMEM((4, 512, 128), BF16), pltpu.VMEM((4, 4, 8, 128), F32),
            pltpu.VMEM((512, 4096), BF16),
            dma((4,)), dma((4,)), dma, dma((3,)), dma, dma,
            dma, dma, dma, dma((3,)), dma, dma, dma((17,)), dma,
        ],
        compiler_params=pltpu.CompilerParams(collective_id=0, has_side_effects=True, vmem_limit_bytes=VMEM_LIMIT),
        name="gather_project",
    )(queries, keys, values, attn, grad_out, w_out)


BLK = 512
SCALE = HDIM ** (-0.5)
LOG2E = 1.4426950408889634


def attn_kernel(first, q, k, v, g, rd, dq, dk, dv, sbuf, dka, dva):
    dka[...] = jnp.zeros_like(dka)
    dva[...] = jnp.zeros_like(dva)
    nb = 2048 // BLK
    for i in range(nb):
        qs = pl.ds(i * BLK, BLK)
        pos = lax.broadcasted_iota(jnp.int32, (1, BLK), 1) + i * BLK
        seg = jnp.zeros((1, BLK), jnp.int32)
        low = jnp.int32(0)
        for e in range(8):
            st = first[0, e]
            seg = jnp.where(pos >= st, jnp.maximum(seg, st), seg)
            low = jnp.where(st <= i * BLK, jnp.maximum(low, st), low)
        jmin = low // BLK
        rdi = jnp.concatenate([rd[i * (BLK // 128) + t][:1] for t in range(BLK // 128)], axis=1)

        def scores(j, m):
            ks = pl.ds(pl.multiple_of(j * BLK, BLK), BLK)
            sc = lax.dot_general(k[ks, :], q[qs, :], NT, preferred_element_type=F32) * (SCALE * LOG2E)
            kp = lax.broadcasted_iota(jnp.int32, (BLK, BLK), 0) + j * BLK
            sc = jnp.where((kp <= pos) & (kp >= seg), sc, -1e30)
            sbuf[ks, :] = sc
            return jnp.maximum(m, jnp.max(sc.reshape(BLK // 8, 8, BLK), axis=0))

        m = lax.fori_loop(jmin, i + 1, scores, jnp.full((8, BLK), -1e30, F32))
        m = jnp.max(m, axis=0, keepdims=True)

        def expo(j, tot):
            ks = pl.ds(pl.multiple_of(j * BLK, BLK), BLK)
            e = jnp.exp2(sbuf[ks, :] - m)
            sbuf[ks, :] = e
            return tot + jnp.sum(e.reshape(BLK // 8, 8, BLK), axis=0)

        tot = lax.fori_loop(jmin, i + 1, expo, jnp.zeros((8, BLK), F32))
        inv = 1.0 / jnp.sum(tot, axis=0, keepdims=True)

        def grads(j, acc):
            ks = pl.ds(pl.multiple_of(j * BLK, BLK), BLK)
            prob = sbuf[ks, :] * inv
            gp = lax.dot_general(v[ks, :], g[qs, :], NT, preferred_element_type=F32)
            ds = (prob * (gp - rdi)).astype(BF16)
            dva[ks, :] += lax.dot_general(prob.astype(BF16), g[qs, :], NN, preferred_element_type=F32)
            dka[ks, :] += lax.dot_general(ds, q[qs, :], NN, preferred_element_type=F32)
            return acc + lax.dot_general(ds, k[ks, :], TN, preferred_element_type=F32)

        acc = lax.fori_loop(jmin, i + 1, grads, jnp.zeros((BLK, HDIM), F32))
        dq[qs, :] = (acc * SCALE).astype(BF16)
    dk[...] = (dka[...] * SCALE).astype(BF16)
    dv[...] = dva[...].astype(BF16)


def attention(first, q, k, v, g, rd):
    vm = pl.BlockSpec(memory_space=pltpu.VMEM)
    head = jax.ShapeDtypeStruct((2048, 128), BF16)
    return pl.pallas_call(
        attn_kernel,
        out_shape=(head, head, head),
        in_specs=[pl.BlockSpec(memory_space=pltpu.SMEM)] + [vm] * 5,
        out_specs=(vm,) * 3,
        scratch_shapes=[pltpu.VMEM((2048, BLK), F32), pltpu.VMEM((2048, HDIM), F32), pltpu.VMEM((2048, HDIM), F32)],
        compiler_params=pltpu.CompilerParams(vmem_limit_bytes=VMEM_LIMIT),
        name="attention_grads",
    )(first, q, k, v, g, rd)


def return_kernel(
    dq, dk, dv, dwp, oq, ok, ov, ow, pbuf, psum, zbuf, h_rs, p_rs, z_rs, h_ss, p_ss, z_ss, loc,
):
    dp, c, s, p, q, block = place()
    bar = pltpu.get_barrier_semaphore()
    for a in range(4):
        for b in range(4):
            if a or b:
                pl.semaphore_signal(
                    bar, 1, device_id=(dp, block((p + a) % 4, (q + b) % 4)), device_id_type=MESH
                )
    for a in range(1, 16):
        pl.semaphore_signal(bar, 1, device_id=((dp + a) % 16, s), device_id_type=MESH)
    lp = pltpu.make_async_copy(dwp.at[rows(p)], pbuf.at[p], loc.at[0])
    lp.start()
    lh = []
    for t, (src, dst) in enumerate(((dq, oq), (dk, ok), (dv, ov))):
        cp = pltpu.make_async_copy(src.at[rows(s)], dst.at[:, rows(s)], loc.at[1 + t])
        cp.start()
        lh.append(cp)
    pl.semaphore_wait(bar, 30)
    for a in (1, 3, 2):
        pp = (p + a) % 4
        remote(dwp.at[rows(pp)], pbuf.at[p], p_ss, p_rs, dp, block(pp, q))
    lp.wait()
    drain(pbuf.at[pl.ds(0, 3)], p_rs)
    for a in range(4):
        for b in range(4):
            if a or b:
                d = block((p + a) % 4, (q + b) % 4)
                for t, (src, dst) in enumerate(((dq, oq), (dk, ok), (dv, ov))):
                    remote(src.at[rows(d)], dst.at[:, rows(s)], h_ss.at[t], h_rs.at[t], dp, d)
    for n in range(16):
        cs = slice(n * 256, (n + 1) * 256)
        tot = pbuf[0, :, cs].astype(F32)
        for a in range(1, 4):
            tot += pbuf[a, :, cs].astype(F32)
        psum[n] = tot.astype(BF16)
    lz = pltpu.make_async_copy(psum.at[dp], zbuf.at[dp], loc.at[4])
    lz.start()
    for a in range(1, 16):
        d = (dp + a) % 16
        remote(psum.at[d], zbuf.at[dp], z_ss, z_rs, d, s)
    lz.wait()
    drain(zbuf.at[pl.ds(0, 15)], z_rs)
    tot = zbuf[0].astype(F32)
    for n in range(1, 16):
        tot += zbuf[n].astype(F32)
    ow[...] = tot
    for cp in lh:
        cp.wait()
    for t, src in enumerate((dq, dk, dv)):
        drain(src.at[pl.ds(0, 1920)], h_rs.at[t])
    drain(pbuf.at[pl.ds(0, 3)], p_ss)
    drain(zbuf.at[pl.ds(0, 15)], z_ss)
    for t, src in enumerate((dq, dk, dv)):
        drain(src.at[pl.ds(0, 1920)], h_ss.at[t])


def give_back(dq, dk, dv, dwp):
    any_ = pl.BlockSpec(memory_space=pl.ANY)
    tok = jax.ShapeDtypeStruct((128, 2048), BF16)
    dma = pltpu.SemaphoreType.DMA
    return pl.pallas_call(
        return_kernel,
        out_shape=(tok, tok, tok, jax.ShapeDtypeStruct((128, 256), F32)),
        in_specs=[any_] * 4,
        out_specs=(any_, any_, any_, pl.BlockSpec(memory_space=pltpu.VMEM)),
        scratch_shapes=[
            pltpu.VMEM((4, 128, 4096), BF16), pltpu.VMEM((16, 128, 256), BF16), pltpu.VMEM((16, 128, 256), BF16),
            dma((3,)), dma, dma, dma((3,)), dma, dma, dma((5,)),
        ],
        compiler_params=pltpu.CompilerParams(collective_id=1, has_side_effects=True, vmem_limit_bytes=VMEM_LIMIT),
        name="return_reduce",
    )(dq, dk, dv, dwp)


def shards(queries, keys, values, attn, grad_out, w_out, starts):
    qh, kh, vh, gh, rdh, dwp = gather(queries, keys, values, attn, grad_out, w_out)
    dq, dk, dv = attention(starts, qh, kh, vh, gh, rdh)
    return give_back(dq, dk, dv, dwp)


def solution(mesh):
    tok = P(("dp", "seq"), None)
    return jax.shard_map(
        shards,
        mesh=mesh,
        in_specs=(tok, tok, tok, tok, tok, P("seq", None), P("dp", None)),
        out_specs=(tok, tok, tok, P("seq", "dp")),
        check_vma=False,
    )
```

```python
import functools

import jax
import jax.numpy as jnp
from jax import lax
from jax.experimental import pallas as pl
from jax.experimental.pallas import tpu as pltpu
from jax.sharding import PartitionSpec as P

HDIM = 128
MESH = pl.DeviceIdType.MESH
BF16 = jnp.bfloat16
F32 = jnp.float32
NT = (((1,), (1,)), ((), ()))
NN = (((1,), (0,)), ((), ()))
TN = (((0,), (0,)), ((), ()))
VMEM_LIMIT = 56 << 20


def place():
    dp = lax.axis_index("dp")
    s = lax.axis_index("seq")
    c = dp % 2
    x, y = s // 4, s % 4
    p = x * (1 - c) + y * c
    q = y * (1 - c) + x * c
    sp, sq = 4 - 3 * c, 1 + 3 * c

    def block(pp, qq):
        return pp * sp + qq * sq

    return dp, c, s, p, q, block


def remote(src, dst, ssem, rsem, dp, s):
    cp = pltpu.make_async_remote_copy(
        src_ref=src, dst_ref=dst, send_sem=ssem, recv_sem=rsem, device_id=(dp, s), device_id_type=MESH
    )
    cp.start()


def drain(ref, sem):
    pltpu.make_async_copy(ref, ref, sem).wait()


def rows(i, n=128):
    return pl.ds(pl.multiple_of(i * n, n), n)


STEPS = 5


def spread(src, buf, me, send, ss, rs):
    nxt, prv = (me + 1) % 4, (me + 3) % 4
    top, low = src.at[pl.ds(0, 64)], src.at[pl.ds(64, 64)]
    send(top, buf.at[rows(me * 2, 64)], ss, rs.at[0], nxt)
    send(low, buf.at[rows(me * 2 + 1, 64)], ss, rs.at[1], prv)
    send(low, buf.at[rows(me * 2 + 1, 64)], ss, rs.at[2], nxt)
    send(top, buf.at[rows(me * 2, 64)], ss, rs.at[3], prv)


def pass_on(buf, me, send, ss, rs):
    nxt, prv = (me + 1) % 4, (me + 3) % 4
    top = buf.at[rows(prv * 2, 64)]
    drain(top, rs.at[0])
    send(top, top, ss, rs.at[4], nxt)
    low = buf.at[rows(nxt * 2 + 1, 64)]
    drain(low, rs.at[1])
    send(low, low, ss, rs.at[5], prv)


def arrive(buf, me, rs):
    nxt, prv, opp = (me + 1) % 4, (me + 3) % 4, (me + 2) % 4
    drain(buf.at[rows(prv * 2 + 1, 64)], rs.at[2])
    drain(buf.at[rows(nxt * 2, 64)], rs.at[3])
    drain(buf.at[rows(opp * 2, 64)], rs.at[4])
    drain(buf.at[rows(opp * 2 + 1, 64)], rs.at[5])


def gather_kernel(
    q_in, k_in, v_in, o_in, g_in, w_in,
    qh, kh, vh, gh, rdh, cur, own,
    gbuf, wbuf, abuf, atbuf, gsnd, rdsnd, dwv, slots,
    g_rs, w_rs, a_rs, h_rs, ga_rs, rd_rs, r_rs,
    g_ss, w_ss, a_ss, h_ss, ga_ss, rd_ss, r_ss, loc,
):
    dp, c, s, p, q, block = place()
    z = dp // 2
    up, down = ((z + 1) % 8) * 2 + c, ((z + 7) % 8) * 2 + c
    bar = pltpu.get_barrier_semaphore()
    for a in range(4):
        for b in range(4):
            if a or b:
                pl.semaphore_signal(
                    bar, 1, device_id=(dp, block((p + a) % 4, (q + b) % 4)), device_id_type=MESH
                )
    pl.semaphore_signal(bar, 1, device_id=(up, s), device_id_type=MESH)
    pl.semaphore_signal(bar, 1, device_id=(down, s), device_id_type=MESH)

    lg = pltpu.make_async_copy(g_in, gbuf.at[rows(q)], loc.at[0])
    lw = pltpu.make_async_copy(w_in, wbuf.at[rows(p)], loc.at[1])
    lg.start()
    lw.start()
    la = []
    for pp in range(4):
        cp = pltpu.make_async_copy(
            o_in.at[:, rows(block(pp, q))], abuf.at[rows(q), pl.ds(pp * 128, 128)], loc.at[2 + pp]
        )
        cp.start()
        la.append(cp)
    heads = ((q_in, qh), (k_in, kh), (v_in, vh))
    lh = []
    for t, (src, dst) in enumerate(heads):
        cp = pltpu.make_async_copy(src.at[:, rows(s)], dst.at[rows(s)], loc.at[6 + t])
        cp.start()
        lh.append(cp)

    def send_q(src, dst, ssem, rsem, qq):
        remote(src, dst, ssem, rsem, dp, block(p, qq))

    def send_p(src, dst, ssem, rsem, pp):
        remote(src, dst, ssem, rsem, dp, block(pp, q))

    def send_heads(t):
        src, dst = heads[t]
        for a in range(4):
            for b in range(4):
                if a or b:
                    d = block((p + a) % 4, (q + b) % 4)
                    remote(src.at[:, rows(d)], dst.at[rows(s)], h_ss.at[t], h_rs.at[t], dp, d)

    def ring_send(t):
        for lane in range(4):
            src = dwv.at[0, lane] if t == 0 else slots.at[t - 1, lane]
            remote(src, slots.at[t, lane], r_ss, r_rs.at[t, lane], up if lane < 2 else down, s)

    def ring_step(t):
        for lane in range(4):
            drain(slots.at[t, lane], r_rs.at[t, lane])
            slots[t, lane] = (slots[t, lane].astype(F32) + dwv[t + 1, lane].astype(F32)).astype(BF16)
            if t < STEPS - 1:
                remote(
                    slots.at[t, lane], slots.at[t + 1, lane], r_ss, r_rs.at[t + 1, lane],
                    up if lane < 2 else down, s,
                )

    pl.semaphore_wait(bar, 17)
    spread(g_in, gbuf, q, send_q, g_ss, g_rs)
    for b in (1, 3, 2):
        qq = (q + b) % 4
        for f in range(4):
            send_q(o_in.at[:, rows(block(f, qq))], abuf.at[rows(q), pl.ds(f * 128, 128)], a_ss, a_rs, qq)
    pass_on(gbuf, q, send_q, g_ss, g_rs)
    spread(w_in, wbuf, p, send_p, w_ss, w_rs)

    for cp in la:
        cp.wait()
    drain(abuf.at[pl.ds(0, 384)], a_rs)
    atbuf[...] = abuf[...].T
    lg.wait()
    arrive(gbuf, q, g_rs)

    def project(n):
        for half, chunk in ((0, (z + 7 - n) % 8), (1, (z + 1 + n) % 8)):
            part = lax.dot_general(
                atbuf[pl.ds(half * 256, 256), :], gbuf[:, rows(chunk, 512)], NN, preferred_element_type=F32
            ).astype(BF16)
            dwv[n, half * 2] = part[:128]
            dwv[n, half * 2 + 1] = part[128:]

    project(0)
    ring_send(0)
    pl.loop(1, 8)(project)
    pass_on(wbuf, p, send_p, w_ss, w_rs)
    send_heads(0)
    ring_step(0)
    lw.wait()
    arrive(wbuf, p, w_rs)
    send_heads(1)
    send_heads(2)

    ones = jnp.ones((8, 128), F32)
    for n in range(2):
        ga = lax.dot_general(
            gbuf[...], wbuf[pl.ds(n * 256, 256), :], NT, preferred_element_type=F32
        ).astype(BF16)
        for m in range(2):
            f = n * 2 + m
            gf = ga[:, m * 128 : (m + 1) * 128]
            gsnd[f] = gf
            prod = gf.astype(F32) * abuf[:, f * 128 : (f + 1) * 128].astype(F32)
            rd = lax.dot_general(ones, prod, NT, preferred_element_type=F32, precision=lax.Precision.HIGHEST)
            for t in range(4):
                rdsnd[f, t] = rd[:, t * 128 : (t + 1) * 128]

    lga = []
    for b in range(4):
        cp = pltpu.make_async_copy(gsnd.at[p, pl.ds(b * 128, 128)], gh.at[rows(block(p, b))], loc.at[9 + b])
        cp.start()
        lga.append(cp)
        cp = pltpu.make_async_copy(rdsnd.at[p, b], rdh.at[block(p, b)], loc.at[13 + b])
        cp.start()
        lga.append(cp)
    for a in (1, 3, 2):
        pp = (p + a) % 4
        for b in range(4):
            send_p(gsnd.at[pp, pl.ds(b * 128, 128)], gh.at[rows(block(p, b))], ga_ss, ga_rs, pp)
            send_p(rdsnd.at[pp, b], rdh.at[block(p, b)], rd_ss, rd_rs, pp)

    lown = pltpu.make_async_copy(dwv.at[pl.ds(STEPS + 1, 7 - STEPS)], own, loc.at[17])
    lown.start()
    for t in range(1, STEPS):
        ring_step(t)
    lcur = pltpu.make_async_copy(slots.at[STEPS - 1], cur, loc.at[18])
    lcur.start()

    for cp in lga:
        cp.wait()
    for cp in lh:
        cp.wait()
    drain(gsnd.at[pl.ds(0, 3)], ga_rs)
    drain(rdsnd.at[pl.ds(0, 3)], rd_rs)
    for t, (src, dst) in enumerate(heads):
        drain(dst.at[pl.ds(0, 1920)], h_rs.at[t])
    lown.wait()
    lcur.wait()
    drain(gbuf.at[pl.ds(0, 384)], g_ss)
    drain(wbuf.at[pl.ds(0, 384)], w_ss)
    drain(abuf.at[pl.ds(0, 384)], a_ss)
    drain(gsnd.at[pl.ds(0, 3)], ga_ss)
    drain(rdsnd.at[pl.ds(0, 3)], rd_ss)
    drain(slots.at[pl.ds(0, STEPS)], r_ss)
    for t, (src, dst) in enumerate(heads):
        drain(dst.at[pl.ds(0, 1920)], h_ss.at[t])


def gather(queries, keys, values, attn, grad_out, w_out):
    any_ = pl.BlockSpec(memory_space=pl.ANY)
    head = jax.ShapeDtypeStruct((2048, 128), BF16)
    dma = pltpu.SemaphoreType.DMA
    return pl.pallas_call(
        gather_kernel,
        out_shape=(head, head, head, head, jax.ShapeDtypeStruct((16, 8, 128), F32),
                   jax.ShapeDtypeStruct((4, 128, 512), BF16),
                   jax.ShapeDtypeStruct((7 - STEPS, 4, 128, 512), BF16)),
        in_specs=[any_] * 6,
        out_specs=(any_,) * 7,
        scratch_shapes=[
            pltpu.VMEM((512, 4096), BF16), pltpu.VMEM((512, 4096), BF16), pltpu.VMEM((512, 512), BF16),
            pltpu.VMEM((512, 512), BF16), pltpu.VMEM((4, 512, 128), BF16), pltpu.VMEM((4, 4, 8, 128), F32),
            pltpu.VMEM((8, 4, 128, 512), BF16), pltpu.VMEM((STEPS, 4, 128, 512), BF16),
            dma((6,)), dma((6,)), dma, dma((3,)), dma, dma, dma((STEPS, 4)),
            dma, dma, dma, dma((3,)), dma, dma, dma, dma((19,)),
        ],
        compiler_params=pltpu.CompilerParams(collective_id=0, has_side_effects=True, vmem_limit_bytes=VMEM_LIMIT),
        name="gather_project",
    )(queries, keys, values, attn, grad_out, w_out)


BLK = 512
SCALE = HDIM ** (-0.5)
LOG2E = 1.4426950408889634


def attn_kernel(first, q, k, v, g, rd, dq, dk, dv, sbuf, dka, dva):
    dka[...] = jnp.zeros_like(dka)
    dva[...] = jnp.zeros_like(dva)
    nb = 2048 // BLK
    for i in range(nb):
        qs = pl.ds(i * BLK, BLK)
        pos = lax.broadcasted_iota(jnp.int32, (1, BLK), 1) + i * BLK
        seg = jnp.zeros((1, BLK), jnp.int32)
        low = jnp.int32(0)
        for e in range(8):
            st = first[0, e]
            seg = jnp.where(pos >= st, jnp.maximum(seg, st), seg)
            low = jnp.where(st <= i * BLK, jnp.maximum(low, st), low)
        jmin = low // BLK
        rdi = jnp.concatenate([rd[i * (BLK // 128) + t][:1] for t in range(BLK // 128)], axis=1)

        def scores(j, m):
            ks = pl.ds(pl.multiple_of(j * BLK, BLK), BLK)
            sc = lax.dot_general(k[ks, :], q[qs, :], NT, preferred_element_type=F32) * (SCALE * LOG2E)
            kp = lax.broadcasted_iota(jnp.int32, (BLK, BLK), 0) + j * BLK
            sc = jnp.where((kp <= pos) & (kp >= seg), sc, -1e30)
            sbuf[ks, :] = sc
            return jnp.maximum(m, jnp.max(sc.reshape(BLK // 8, 8, BLK), axis=0))

        m = lax.fori_loop(jmin, i + 1, scores, jnp.full((8, BLK), -1e30, F32))
        m = jnp.max(m, axis=0, keepdims=True)

        def expo(j, tot):
            ks = pl.ds(pl.multiple_of(j * BLK, BLK), BLK)
            e = jnp.exp2(sbuf[ks, :] - m)
            sbuf[ks, :] = e
            return tot + jnp.sum(e.reshape(BLK // 8, 8, BLK), axis=0)

        tot = lax.fori_loop(jmin, i + 1, expo, jnp.zeros((8, BLK), F32))
        inv = 1.0 / jnp.sum(tot, axis=0, keepdims=True)

        def grads(j, acc):
            ks = pl.ds(pl.multiple_of(j * BLK, BLK), BLK)
            prob = sbuf[ks, :] * inv
            gp = lax.dot_general(v[ks, :], g[qs, :], NT, preferred_element_type=F32)
            ds = (prob * (gp - rdi)).astype(BF16)
            dva[ks, :] += lax.dot_general(prob.astype(BF16), g[qs, :], NN, preferred_element_type=F32)
            dka[ks, :] += lax.dot_general(ds, q[qs, :], NN, preferred_element_type=F32)
            return acc + lax.dot_general(ds, k[ks, :], TN, preferred_element_type=F32)

        acc = lax.fori_loop(jmin, i + 1, grads, jnp.zeros((BLK, HDIM), F32))
        dq[qs, :] = (acc * SCALE).astype(BF16)
    dk[...] = (dka[...] * SCALE).astype(BF16)
    dv[...] = dva[...].astype(BF16)


def attention(first, q, k, v, g, rd):
    vm = pl.BlockSpec(memory_space=pltpu.VMEM)
    head = jax.ShapeDtypeStruct((2048, 128), BF16)
    return pl.pallas_call(
        attn_kernel,
        out_shape=(head, head, head),
        in_specs=[pl.BlockSpec(memory_space=pltpu.SMEM)] + [vm] * 5,
        out_specs=(vm,) * 3,
        scratch_shapes=[pltpu.VMEM((2048, BLK), F32), pltpu.VMEM((2048, HDIM), F32), pltpu.VMEM((2048, HDIM), F32)],
        compiler_params=pltpu.CompilerParams(vmem_limit_bytes=VMEM_LIMIT),
        name="attention_grads",
    )(first, q, k, v, g, rd)


def return_kernel(
    dq, dk, dv, cur, own_in, oq, ok, ov, ow,
    own, slots, pbuf, csnd, cbuf, h_rs, r_rs, p_rs, c_rs, h_ss, r_ss, p_ss, c_ss, loc,
):
    dp, c, s, p, q, block = place()
    z = dp // 2
    up, down = ((z + 1) % 8) * 2 + c, ((z + 7) % 8) * 2 + c
    mate = z * 2 + 1 - c
    bar = pltpu.get_barrier_semaphore()
    for a in range(4):
        for b in range(4):
            if a or b:
                pl.semaphore_signal(
                    bar, 1, device_id=(dp, block((p + a) % 4, (q + b) % 4)), device_id_type=MESH
                )
    for d in (up, down, mate):
        pl.semaphore_signal(bar, 1, device_id=(d, s), device_id_type=MESH)
    lo = pltpu.make_async_copy(own_in, own, loc.at[0])
    lo.start()
    heads = ((dq, oq), (dk, ok), (dv, ov))
    lh = []
    for t, (src, dst) in enumerate(heads):
        cp = pltpu.make_async_copy(src.at[rows(s)], dst.at[:, rows(s)], loc.at[1 + t])
        cp.start()
        lh.append(cp)
    pl.semaphore_wait(bar, 18)
    left = 7 - STEPS
    for lane in range(4):
        remote(cur.at[lane], slots.at[0, lane], r_ss, r_rs.at[0, lane], up if lane < 2 else down, s)
    for a in range(4):
        for b in range(4):
            if a or b:
                d = block((p + a) % 4, (q + b) % 4)
                for t, (src, dst) in enumerate(heads):
                    remote(src.at[rows(d)], dst.at[:, rows(s)], h_ss.at[t], h_rs.at[t], dp, d)
    lo.wait()
    for t in range(left):
        for lane in range(4):
            drain(slots.at[t, lane], r_rs.at[t, lane])
            slots[t, lane] = (slots[t, lane].astype(F32) + own[t, lane].astype(F32)).astype(BF16)
            if t < left - 1:
                remote(
                    slots.at[t, lane], slots.at[t + 1, lane], r_ss, r_rs.at[t + 1, lane],
                    up if lane < 2 else down, s,
                )
    lp = pltpu.make_async_copy(slots.at[left - 1, p], pbuf.at[p], loc.at[4])
    lp.start()
    for a in (1, 3, 2):
        pp = (p + a) % 4
        remote(slots.at[left - 1, pp], pbuf.at[p], p_ss, p_rs, dp, block(pp, q))
    lp.wait()
    drain(pbuf.at[pl.ds(0, 3)], p_rs)
    tot = pbuf[0].astype(F32)
    for a in range(1, 4):
        tot += pbuf[a].astype(F32)
    csnd[0] = tot[:, :256]
    csnd[1] = tot[:, 256:]
    remote(csnd.at[1 - c], cbuf, c_ss, c_rs, mate, s)
    drain(cbuf, c_rs)
    ow[...] = csnd[c] + cbuf[...]
    for cp in lh:
        cp.wait()
    for t, (src, dst) in enumerate(heads):
        drain(src.at[pl.ds(0, 1920)], h_rs.at[t])
    drain(slots, r_ss)
    drain(pbuf.at[pl.ds(0, 3)], p_ss)
    drain(cbuf, c_ss)
    for t, (src, dst) in enumerate(heads):
        drain(src.at[pl.ds(0, 1920)], h_ss.at[t])


def give_back(dq, dk, dv, cur, own):
    any_ = pl.BlockSpec(memory_space=pl.ANY)
    tok = jax.ShapeDtypeStruct((128, 2048), BF16)
    dma = pltpu.SemaphoreType.DMA
    left = 7 - STEPS
    return pl.pallas_call(
        return_kernel,
        out_shape=(tok, tok, tok, jax.ShapeDtypeStruct((128, 256), F32)),
        in_specs=[any_] * 5,
        out_specs=(any_, any_, any_, pl.BlockSpec(memory_space=pltpu.VMEM)),
        scratch_shapes=[
            pltpu.VMEM((left, 4, 128, 512), BF16), pltpu.VMEM((left, 4, 128, 512), BF16),
            pltpu.VMEM((4, 128, 512), BF16), pltpu.VMEM((2, 128, 256), F32), pltpu.VMEM((128, 256), F32),
            dma((3,)), dma((left, 4)), dma, dma, dma((3,)), dma, dma, dma, dma((5,)),
        ],
        compiler_params=pltpu.CompilerParams(collective_id=1, has_side_effects=True, vmem_limit_bytes=VMEM_LIMIT),
        name="return_reduce",
    )(dq, dk, dv, cur, own)


def finish_kernel(*refs):
    n = len(refs) // 2
    for i in range(n):
        refs[n + i][...] = refs[i][...]


def finish(*arrays):
    vm = pl.BlockSpec(memory_space=pltpu.VMEM)
    return pl.pallas_call(
        finish_kernel,
        out_shape=tuple(jax.ShapeDtypeStruct(a.shape, a.dtype) for a in arrays),
        in_specs=[vm] * len(arrays),
        out_specs=(vm,) * len(arrays),
        name="finish",
    )(*arrays)


def shards(queries, keys, values, attn, grad_out, w_out, starts):
    qh, kh, vh, gh, rdh, cur, own = gather(queries, keys, values, attn, grad_out, w_out)
    dq, dk, dv = attention(starts, qh, kh, vh, gh, rdh)
    return finish(*give_back(dq, dk, dv, cur, own))


def solution(mesh):
    tok = P(("dp", "seq"), None)
    return jax.shard_map(
        shards,
        mesh=mesh,
        in_specs=(tok, tok, tok, tok, tok, P("seq", None), P("dp", None)),
        out_specs=(tok, tok, tok, P("seq", "dp")),
        check_vma=False,
    )
```

```python
import functools

import jax
import jax.numpy as jnp
from jax import lax
from jax.experimental import pallas as pl
from jax.experimental.pallas import tpu as pltpu
from jax.sharding import PartitionSpec as P

HDIM = 128
MESH = pl.DeviceIdType.MESH
BF16 = jnp.bfloat16
F32 = jnp.float32
NT = (((1,), (1,)), ((), ()))
NN = (((1,), (0,)), ((), ()))
TN = (((0,), (0,)), ((), ()))
VMEM_LIMIT = 56 << 20


def place():
    dp = lax.axis_index("dp")
    s = lax.axis_index("seq")
    c = dp % 2
    x, y = s // 4, s % 4
    p = x * (1 - c) + y * c
    q = y * (1 - c) + x * c
    sp, sq = 4 - 3 * c, 1 + 3 * c

    def block(pp, qq):
        return pp * sp + qq * sq

    return dp, c, s, p, q, block


def remote(src, dst, ssem, rsem, dp, s):
    cp = pltpu.make_async_remote_copy(
        src_ref=src, dst_ref=dst, send_sem=ssem, recv_sem=rsem, device_id=(dp, s), device_id_type=MESH
    )
    cp.start()


def drain(ref, sem):
    pltpu.make_async_copy(ref, ref, sem).wait()


def rows(i, n=128):
    return pl.ds(pl.multiple_of(i * n, n), n)


BLK = 512
NBLK = 2048 // BLK
SCALE = HDIM ** (-0.5)
LOG2E = 1.4426950408889634


def spread(pieces, me, send_next, send_prev, ss, rs):
    for half, send, sem in ((0, send_next, 0), (1, send_prev, 1), (1, send_next, 2), (0, send_prev, 3)):
        for src, dst in pieces(me, half):
            send(src, dst, ss, rs.at[sem])


def pass_on(pieces, whole, me, send_next, send_prev, ss, rs):
    nxt, prv = (me + 1) % 4, (me + 3) % 4
    drain(whole, rs.at[0])
    for _, ref in pieces(prv, 0):
        send_next(ref, ref, ss, rs.at[4])
    drain(whole, rs.at[1])
    for _, ref in pieces(nxt, 1):
        send_prev(ref, ref, ss, rs.at[5])


def arrive(whole, rs):
    for sem in (2, 3, 4, 5):
        drain(whole, rs.at[sem])


def attend(i, first, q, k, v, g, rd, dq, sbuf, dka, dva):
    qs = pl.ds(i * BLK, BLK)
    pos = lax.broadcasted_iota(jnp.int32, (1, BLK), 1) + i * BLK
    seg = jnp.zeros((1, BLK), jnp.int32)
    for e in range(8):
        st = first[0, e]
        seg = jnp.where(pos >= st, jnp.maximum(seg, st), seg)
    rdi = jnp.concatenate([rd[i * (BLK // 128) + t][:1] for t in range(BLK // 128)], axis=1)

    def scores(j, m):
        ks = pl.ds(pl.multiple_of(j * BLK, BLK), BLK)
        sc = lax.dot_general(k[ks, :], q[qs, :], NT, preferred_element_type=F32) * (SCALE * LOG2E)
        kp = lax.broadcasted_iota(jnp.int32, (BLK, BLK), 0) + j * BLK
        sc = jnp.where((kp <= pos) & (kp >= seg), sc, -1e30)
        sbuf[ks, :] = sc
        return jnp.maximum(m, jnp.max(sc.reshape(BLK // 8, 8, BLK), axis=0))

    m = lax.fori_loop(0, i + 1, scores, jnp.full((8, BLK), -1e30, F32))
    m = jnp.max(m, axis=0, keepdims=True)

    def expo(j, tot):
        ks = pl.ds(pl.multiple_of(j * BLK, BLK), BLK)
        e = jnp.exp2(sbuf[ks, :] - m)
        sbuf[ks, :] = e
        return tot + jnp.sum(e.reshape(BLK // 8, 8, BLK), axis=0)

    tot = lax.fori_loop(0, i + 1, expo, jnp.zeros((8, BLK), F32))
    inv = 1.0 / jnp.sum(tot, axis=0, keepdims=True)

    def grads(j, acc):
        ks = pl.ds(pl.multiple_of(j * BLK, BLK), BLK)
        prob = sbuf[ks, :] * inv
        gp = lax.dot_general(v[ks, :], g[qs, :], NT, preferred_element_type=F32)
        ds = (prob * (gp - rdi)).astype(BF16)
        dva[ks, :] += lax.dot_general(prob.astype(BF16), g[qs, :], NN, preferred_element_type=F32)
        dka[ks, :] += lax.dot_general(ds, q[qs, :], NN, preferred_element_type=F32)
        return acc + lax.dot_general(ds, k[ks, :], TN, preferred_element_type=F32)

    acc = lax.fori_loop(0, i + 1, grads, jnp.zeros((BLK, HDIM), F32))
    dq[qs, :] = (acc * SCALE).astype(BF16)


def whole_kernel(
    q_in, k_in, v_in, o_in, g_in, w_in, first,
    oq, ok, ov, ow,
    gbuf, wbuf, abuf, atbuf, gsnd, rdsnd, dwv, slots, qh, kh, vh, gh, rdh,
    sbuf, dka, dva, dq, dk, dv, pbuf, csnd, cbuf,
    g_rs, wx_rs, wz_rs, a_rs, h_rs, ga_rs, rd_rs, r_rs, b_rs, p_rs, c_rs,
    g_ss, wx_ss, wz_ss, a_ss, h_ss, ga_ss, rd_ss, r_ss, b_ss, p_ss, c_ss,
    loc, ga_loc, rd_loc, b_loc,
):
    dp, c, s, p, q, block = place()
    z = dp // 2
    zq = z % 4
    up, down = ((z + 1) % 8) * 2 + c, ((z + 7) % 8) * 2 + c
    mate = z * 2 + 1 - c
    bar = pltpu.get_barrier_semaphore()
    for a in range(4):
        for b in range(4):
            if a or b:
                pl.semaphore_signal(
                    bar, 1, device_id=(dp, block((p + a) % 4, (q + b) % 4)), device_id_type=MESH
                )
    for d in (up, down, mate):
        pl.semaphore_signal(bar, 1, device_id=(d, s), device_id_type=MESH)

    lg = pltpu.make_async_copy(g_in, gbuf.at[rows(q)], loc.at[0])
    lw = pltpu.make_async_copy(w_in, wbuf.at[rows(p)], loc.at[1])
    lg.start()
    lw.start()
    la = []
    for pp in range(4):
        cp = pltpu.make_async_copy(
            o_in.at[:, rows(block(pp, q))], abuf.at[rows(q), pl.ds(pp * 128, 128)], loc.at[2 + pp]
        )
        cp.start()
        la.append(cp)
    heads = ((q_in, qh), (k_in, kh), (v_in, vh))
    lh = []
    for t, (src, dst) in enumerate(heads):
        cp = pltpu.make_async_copy(src.at[:, rows(s)], dst.at[rows(s)], loc.at[6 + t])
        cp.start()
        lh.append(cp)

    def to_next(src, dst, ssem, rsem):
        remote(src, dst, ssem, rsem, dp, block(p, (q + 1) % 4))

    def to_prev(src, dst, ssem, rsem):
        remote(src, dst, ssem, rsem, dp, block(p, (q + 3) % 4))

    def to_up(src, dst, ssem, rsem):
        remote(src, dst, ssem, rsem, up, s)

    def to_down(src, dst, ssem, rsem):
        remote(src, dst, ssem, rsem, down, s)

    def g_pieces(who, half):
        ref = gbuf.at[rows(who * 2 + half, 64)]
        return [(g_in.at[pl.ds(half * 64, 64)], ref)]

    def w_pieces(who, half):
        refs = [wbuf.at[rows(((p + a) % 4) * 8 + who * 2 + half, 16)] for a in range(1, 4)]
        return [(ref, ref) for ref in refs]

    g_half, w_half = gbuf.at[pl.ds(0, 64)], wbuf.at[pl.ds(0, 48)]

    def send_heads(t):
        src, dst = heads[t]
        for a in range(4):
            for b in range(4):
                if a or b:
                    d = block((p + a) % 4, (q + b) % 4)
                    remote(src.at[:, rows(d)], dst.at[rows(s)], h_ss.at[t], h_rs.at[t], dp, d)

    def ring_send():
        for lane in range(4):
            remote(dwv.at[0, lane], slots.at[0, lane], r_ss, r_rs.at[0, lane], up if lane < 2 else down, s)

    def ring_step(t):
        for lane in (0, 2, 1, 3):
            drain(slots.at[t, lane], r_rs.at[t, lane])
            slots[t, lane] = (slots[t, lane].astype(F32) + dwv[t + 1, lane].astype(F32)).astype(BF16)
            if t < 6:
                remote(
                    slots.at[t, lane], slots.at[t + 1, lane], r_ss, r_rs.at[t + 1, lane],
                    up if lane < 2 else down, s,
                )

    def project(n):
        for half, chunk in ((0, (z + 7 - n) % 8), (1, (z + 1 + n) % 8)):
            part = lax.dot_general(
                atbuf[pl.ds(half * 256, 256), :], gbuf[:, rows(chunk, 512)], NN, preferred_element_type=F32
            ).astype(BF16)
            dwv[n, half * 2] = part[:128]
            dwv[n, half * 2 + 1] = part[128:]

    pl.semaphore_wait(bar, 18)
    for a in (1, 3, 2):
        pp = (p + a) % 4
        remote(
            w_in.at[rows(zq, 32)], wbuf.at[rows(p * 4 + zq, 32)], wx_ss, wx_rs.at[p], dp, block(pp, q)
        )
    spread(g_pieces, q, to_next, to_prev, g_ss, g_rs)
    for b in (1, 3, 2):
        qq = (q + b) % 4
        for f in range(4):
            remote(
                o_in.at[:, rows(block(f, qq))], abuf.at[rows(q), pl.ds(f * 128, 128)], a_ss, a_rs, dp, block(p, qq)
            )
    for a in (1, 3, 2):
        pp = (p + a) % 4
        drain(wbuf.at[rows(pp * 4 + zq, 32)], wx_rs.at[pp])
    spread(w_pieces, zq, to_up, to_down, wz_ss, wz_rs)
    pass_on(g_pieces, g_half, q, to_next, to_prev, g_ss, g_rs)
    send_heads(0)
    for cp in la:
        cp.wait()
    drain(abuf.at[pl.ds(0, 384)], a_rs)
    atbuf[...] = abuf[...].T
    pass_on(w_pieces, w_half, zq, to_up, to_down, wz_ss, wz_rs)
    lg.wait()
    arrive(g_half, g_rs)
    send_heads(1)
    send_heads(2)
    pl.loop(0, 8)(project)
    lw.wait()
    arrive(w_half, wz_rs)
    ring_send()

    for n in range(2):
        ga = lax.dot_general(
            gbuf[...], wbuf[pl.ds(n * 256, 256), :], NT, preferred_element_type=F32
        ).astype(BF16)
        for m in range(2):
            f = n * 2 + m
            gf = ga[:, m * 128 : (m + 1) * 128]
            gsnd[f] = gf
            prod = gf.astype(F32) * abuf[:, f * 128 : (f + 1) * 128].astype(F32)
            rd = jnp.sum(prod.T, axis=0, keepdims=True)
            for t in range(4):
                rdsnd[f, t] = jnp.broadcast_to(rd[:, t * 128 : (t + 1) * 128], (8, 128))

            @pl.when(p == f)
            def _():
                for b in range(4):
                    pltpu.make_async_copy(gsnd.at[f, pl.ds(b * 128, 128)], gh.at[rows(block(p, b))], ga_loc).start()
                    pltpu.make_async_copy(rdsnd.at[f, b], rdh.at[block(p, b)], rd_loc).start()

            @pl.when(p != f)
            def _():
                for b in range(4):
                    remote(
                        gsnd.at[f, pl.ds(b * 128, 128)], gh.at[rows(block(p, b))], ga_ss, ga_rs, dp, block(f, q)
                    )
                    remote(rdsnd.at[f, b], rdh.at[block(p, b)], rd_ss, rd_rs, dp, block(f, q))

    ring_step(0)
    dka[...] = jnp.zeros_like(dka)
    dva[...] = jnp.zeros_like(dva)
    for cp in lh:
        cp.wait()
    drain(gsnd.at[0], ga_loc)
    drain(rdsnd.at[0], rd_loc)
    for t, (src, dst) in enumerate(heads):
        drain(dst.at[pl.ds(0, 1920)], h_rs.at[t])
    drain(gsnd.at[pl.ds(0, 3)], ga_rs)
    drain(rdsnd.at[pl.ds(0, 3)], rd_rs)
    ring_step(1)

    back = ((dq, oq), (dk, ok), (dv, ov))
    for i in range(NBLK - 1, -1, -1):
        attend(i, first, qh, kh, vh, gh, rdh, dq, sbuf, dka, dva)
        qs = pl.ds(i * BLK, BLK)
        dk[qs, :] = (dka[qs, :] * SCALE).astype(BF16)
        dv[qs, :] = dva[qs, :].astype(BF16)
        for t in range(4):
            d = i * 4 + (s + t) % 4

            @pl.when(d == s)
            def _():
                for n, (src, dst) in enumerate(back):
                    pltpu.make_async_copy(src.at[rows(d)], dst.at[:, rows(s)], b_loc.at[n]).start()

            @pl.when(d != s)
            def _():
                for n, (src, dst) in enumerate(back):
                    remote(src.at[rows(d)], dst.at[:, rows(s)], b_ss.at[n], b_rs.at[n], dp, d)
        if i in (3, 2, 0):
            ring_step({3: 2, 2: 3, 0: 4}[i])
    ring_step(5)
    ring_step(6)

    lp = pltpu.make_async_copy(slots.at[6, p], pbuf.at[p], loc.at[9])
    lp.start()
    for a in (1, 3, 2):
        pp = (p + a) % 4
        remote(slots.at[6, pp], pbuf.at[p], p_ss, p_rs, dp, block(pp, q))
    lp.wait()
    drain(pbuf.at[pl.ds(0, 3)], p_rs)
    tot = pbuf[0].astype(F32)
    for a in range(1, 4):
        tot += pbuf[a].astype(F32)
    csnd[0] = tot[:, :256]
    csnd[1] = tot[:, 256:]
    remote(csnd.at[1 - c], cbuf, c_ss, c_rs, mate, s)
    drain(cbuf, c_rs)
    ow[...] = csnd[c] + cbuf[...]

    for n, (src, dst) in enumerate(back):
        drain(src.at[pl.ds(0, 128)], b_loc.at[n])
        drain(src.at[pl.ds(0, 1920)], b_rs.at[n])
        drain(src.at[pl.ds(0, 1920)], b_ss.at[n])
    drain(gbuf.at[pl.ds(0, 384)], g_ss)
    drain(wbuf.at[pl.ds(0, 96)], wx_ss)
    drain(wbuf.at[pl.ds(0, 288)], wz_ss)
    drain(abuf.at[pl.ds(0, 384)], a_ss)
    drain(gsnd.at[pl.ds(0, 3)], ga_ss)
    drain(rdsnd.at[pl.ds(0, 3)], rd_ss)
    drain(slots, r_ss)
    drain(pbuf.at[pl.ds(0, 3)], p_ss)
    drain(cbuf, c_ss)
    for t, (src, dst) in enumerate(heads):
        drain(dst.at[pl.ds(0, 1920)], h_ss.at[t])


def run_whole(queries, keys, values, attn, grad_out, w_out, starts):
    any_ = pl.BlockSpec(memory_space=pl.ANY)
    tok = jax.ShapeDtypeStruct((128, 2048), BF16)
    dma = pltpu.SemaphoreType.DMA
    head = pltpu.VMEM((2048, HDIM), BF16)
    acc = pltpu.VMEM((2048, HDIM), F32)
    return pl.pallas_call(
        whole_kernel,
        out_shape=(tok, tok, tok, jax.ShapeDtypeStruct((128, 256), F32)),
        in_specs=[any_] * 6 + [pl.BlockSpec(memory_space=pltpu.SMEM)],
        out_specs=(any_, any_, any_, pl.BlockSpec(memory_space=pltpu.VMEM)),
        scratch_shapes=[
            pltpu.VMEM((512, 4096), BF16), pltpu.VMEM((512, 4096), BF16), pltpu.VMEM((512, 512), BF16),
            pltpu.VMEM((512, 512), BF16), pltpu.VMEM((4, 512, 128), BF16), pltpu.VMEM((4, 4, 8, 128), F32),
            pltpu.VMEM((8, 4, 128, 512), BF16), pltpu.VMEM((7, 4, 128, 512), BF16),
            head, head, head, head, pltpu.VMEM((16, 8, 128), F32),
            pltpu.VMEM((2048, BLK), F32), acc, acc, head, head, head,
            pltpu.VMEM((4, 128, 512), BF16), pltpu.VMEM((2, 128, 256), F32), pltpu.VMEM((128, 256), F32),
            dma((6,)), dma((4,)), dma((6,)), dma, dma((3,)), dma, dma, dma((7, 4)), dma((3,)), dma, dma,
            dma, dma, dma, dma, dma((3,)), dma, dma, dma, dma((3,)), dma, dma,
            dma((10,)), dma, dma, dma((3,)),
        ],
        compiler_params=pltpu.CompilerParams(collective_id=0, has_side_effects=True, vmem_limit_bytes=VMEM_LIMIT),
        name="whole",
    )(queries, keys, values, attn, grad_out, w_out, starts)


def finish_kernel(*refs):
    n = len(refs) // 2
    for i in range(n):
        refs[n + i][...] = refs[i][...]


def finish(*arrays):
    vm = pl.BlockSpec(memory_space=pltpu.VMEM)
    return pl.pallas_call(
        finish_kernel,
        out_shape=tuple(jax.ShapeDtypeStruct(a.shape, a.dtype) for a in arrays),
        in_specs=[vm] * len(arrays),
        out_specs=(vm,) * len(arrays),
        name="finish",
    )(*arrays)


def shards(queries, keys, values, attn, grad_out, w_out, starts):
    return finish(*run_whole(queries, keys, values, attn, grad_out, w_out, starts))


def solution(mesh):
    tok = P(("dp", "seq"), None)
    return jax.shard_map(
        shards,
        mesh=mesh,
        in_specs=(tok, tok, tok, tok, tok, P("seq", None), P("dp", None)),
        out_specs=(tok, tok, tok, P("seq", "dp")),
        check_vma=False,
    )
```

```python
import functools

import jax
import jax.numpy as jnp
from jax import lax
from jax.experimental import pallas as pl
from jax.experimental.pallas import tpu as pltpu
from jax.sharding import PartitionSpec as P

HDIM = 128
MESH = pl.DeviceIdType.MESH
BF16 = jnp.bfloat16
F32 = jnp.float32
NT = (((1,), (1,)), ((), ()))
NN = (((1,), (0,)), ((), ()))
TN = (((0,), (0,)), ((), ()))
VMEM_LIMIT = 56 << 20


def place():
    dp = lax.axis_index("dp")
    s = lax.axis_index("seq")
    c = dp % 2
    x, y = s // 4, s % 4
    p = x * (1 - c) + y * c
    q = y * (1 - c) + x * c
    sp, sq = 4 - 3 * c, 1 + 3 * c

    def block(pp, qq):
        return pp * sp + qq * sq

    return dp, c, s, p, q, block


def remote(src, dst, ssem, rsem, dp, s):
    cp = pltpu.make_async_remote_copy(
        src_ref=src, dst_ref=dst, send_sem=ssem, recv_sem=rsem, device_id=(dp, s), device_id_type=MESH
    )
    cp.start()


def drain(ref, sem):
    pltpu.make_async_copy(ref, ref, sem).wait()


def rows(i, n=128):
    return pl.ds(pl.multiple_of(i * n, n), n)


BLK = 512
NBLK = 2048 // BLK
SCALE = HDIM ** (-0.5)
LOG2E = 1.4426950408889634
FIRST_STEPS = 3
LAST_STEPS = 2


def spread(pieces, me, send_next, send_prev, ss, rs):
    for half, send, sem in ((0, send_next, 0), (1, send_prev, 1), (1, send_next, 2), (0, send_prev, 3)):
        for src, dst in pieces(me, half):
            send(src, dst, ss, rs.at[sem])


def pass_on(pieces, whole, me, send_next, send_prev, ss, rs):
    nxt, prv = (me + 1) % 4, (me + 3) % 4
    drain(whole, rs.at[0])
    for _, ref in pieces(prv, 0):
        send_next(ref, ref, ss, rs.at[4])
    drain(whole, rs.at[1])
    for _, ref in pieces(nxt, 1):
        send_prev(ref, ref, ss, rs.at[5])


def arrive(whole, rs, sems=(2, 3, 4, 5)):
    for sem in sems:
        drain(whole, rs.at[sem])


def attend(i, first, q, k, v, g, rd, dq, sbuf, dka, dva, between):
    qs = pl.ds(i * BLK, BLK)
    pos = lax.broadcasted_iota(jnp.int32, (1, BLK), 1) + i * BLK
    seg = jnp.zeros((1, BLK), jnp.int32)
    for e in range(8):
        st = first[0, e]
        seg = jnp.where(pos >= st, jnp.maximum(seg, st), seg)
    rdi = jnp.concatenate([rd[i * (BLK // 128) + t][:1] for t in range(BLK // 128)], axis=1)

    def scores(j, m):
        ks = pl.ds(j * BLK, BLK)
        sc = lax.dot_general(k[ks, :], q[qs, :], NT, preferred_element_type=F32) * (SCALE * LOG2E)
        kp = lax.broadcasted_iota(jnp.int32, (BLK, BLK), 0)
        live = kp >= seg - j * BLK
        if j == i:
            live = live & (kp <= pos - j * BLK)
        sc = jnp.where(live, sc, -1e30)
        sbuf[ks, :] = sc
        return jnp.maximum(m, jnp.max(sc.reshape(BLK // 8, 8, BLK), axis=0))

    m = jnp.full((8, BLK), -1e30, F32)
    for j in range(i + 1):
        m = scores(j, m)
    m = jnp.max(m, axis=0, keepdims=True)

    def expo(j, tot):
        ks = pl.ds(j * BLK, BLK)
        e = jnp.exp2(sbuf[ks, :] - m)
        sbuf[ks, :] = e
        return tot + jnp.sum(e.reshape(BLK // 8, 8, BLK), axis=0)

    tot = jnp.zeros((8, BLK), F32)
    for j in range(i + 1):
        tot = expo(j, tot)
    inv = 1.0 / jnp.sum(tot, axis=0, keepdims=True)
    between()

    def grads(j, acc):
        ks = pl.ds(j * BLK, BLK)
        prob = sbuf[ks, :] * inv
        gp = lax.dot_general(v[ks, :], g[qs, :], NT, preferred_element_type=F32)
        ds = (prob * (gp - rdi)).astype(BF16)
        dva[ks, :] += lax.dot_general(prob.astype(BF16), g[qs, :], NN, preferred_element_type=F32)
        dka[ks, :] += lax.dot_general(ds, q[qs, :], NN, preferred_element_type=F32)
        return acc + lax.dot_general(ds, k[ks, :], TN, preferred_element_type=F32)

    acc = jnp.zeros((BLK, HDIM), F32)
    for j in range(i + 1):
        acc = grads(j, acc)
    dq[qs, :] = (acc * SCALE).astype(BF16)


def whole_kernel(
    q_in, k_in, v_in, o_in, g_in, w_in, first,
    oq, ok, ov, ow,
    gbuf, wbuf, gacc, abuf, atbuf, gsnd, rdsnd, dwv, slots, qh, kh, vh, gh, rdh,
    sbuf, dka, dva, dq, dk, dv, tbuf,
    g_rs, wx_rs, wz_rs, a_rs, h_rs, ga_rs, rd_rs, r_rs, b_rs, t_rs,
    g_ss, wx_ss, wz_ss, a_ss, h_ss, ga_ss, rd_ss, r_ss, b_ss, t_ss,
    loc, ga_loc, rd_loc, b_loc, t_loc,
):
    dp, c, s, p, q, block = place()
    z = dp // 2
    zq = z % 4
    up, down = ((z + 1) % 8) * 2 + c, ((z + 7) % 8) * 2 + c
    mate = z * 2 + 1 - c
    bar = pltpu.get_barrier_semaphore()
    for a in range(4):
        for b in range(4):
            if a or b:
                pl.semaphore_signal(
                    bar, 1, device_id=(dp, block((p + a) % 4, (q + b) % 4)), device_id_type=MESH
                )
    for d in (up, down, mate):
        pl.semaphore_signal(bar, 1, device_id=(d, s), device_id_type=MESH)
    for a in range(1, 4):
        pl.semaphore_signal(bar, 1, device_id=(mate, block(p, (q + a) % 4)), device_id_type=MESH)

    lg = pltpu.make_async_copy(g_in, gbuf.at[rows(q)], loc.at[0])
    lw = pltpu.make_async_copy(w_in, wbuf.at[rows(p)], loc.at[1])
    lg.start()
    lw.start()
    la = []
    for pp in range(4):
        cp = pltpu.make_async_copy(
            o_in.at[:, rows(block(pp, q))], abuf.at[rows(q), pl.ds(pp * 128, 128)], loc.at[2 + pp]
        )
        cp.start()
        la.append(cp)
    heads = ((q_in, qh), (k_in, kh), (v_in, vh))
    lh = []
    for t, (src, dst) in enumerate(heads):
        cp = pltpu.make_async_copy(src.at[:, rows(s)], dst.at[rows(s)], loc.at[6 + t])
        cp.start()
        lh.append(cp)

    def to_next(src, dst, ssem, rsem):
        remote(src, dst, ssem, rsem, dp, block(p, (q + 1) % 4))

    def to_prev(src, dst, ssem, rsem):
        remote(src, dst, ssem, rsem, dp, block(p, (q + 3) % 4))

    def to_up(src, dst, ssem, rsem):
        remote(src, dst, ssem, rsem, up, s)

    def to_down(src, dst, ssem, rsem):
        remote(src, dst, ssem, rsem, down, s)

    def g_pieces(who, half):
        ref = gbuf.at[rows(who * 2 + half, 64)]
        return [(g_in.at[pl.ds(half * 64, 64)], ref)]

    def w_pieces(who, half):
        refs = [wbuf.at[rows(((p + a) % 4) * 2 + half, 64), rows(who, 1024)] for a in range(1, 4)]
        return [(ref, ref) for ref in refs]

    g_half, w_half = gbuf.at[pl.ds(0, 64)], wbuf.at[pl.ds(0, 192), pl.ds(0, 1024)]

    def send_heads(t):
        src, dst = heads[t]
        for a in range(4):
            for b in range(4):
                if a or b:
                    d = block((p + a) % 4, (q + b) % 4)
                    remote(src.at[:, rows(d)], dst.at[rows(s)], h_ss.at[t], h_rs.at[t], dp, d)

    def ring_put(way, step, lane, src):
        remote(src, slots.at[way, step, lane], r_ss, r_rs.at[way, step, lane], (up, down)[way], s)

    def ring_begin():
        for lane in range(2):
            ring_put(0, 0, lane, dwv.at[4, lane])
            ring_put(1, 0, lane + 2, dwv.at[4, lane + 2])
        for lane in range(2):
            ring_put(0, 1, lane + 2, dwv.at[3, lane + 2])
            ring_put(1, 1, lane, dwv.at[5, lane])

    def ring_step(step, lanes):
        for way, lane in enumerate(lanes):
            got = slots.at[way, step, lane]
            drain(got, r_rs.at[way, step, lane])
            ahead = (3 - step, 5 + step)[way]
            slots[way, step, lane] = (got[...].astype(F32) + dwv[ahead, lane].astype(F32)).astype(BF16)
            ring_put(way, step + 1, lane, got)

    def project(rel):
        part = lax.dot_general(
            atbuf[...], gbuf[:, rows((z + rel) % 8, 512)], NN, preferred_element_type=F32
        ).astype(BF16)
        for lane in range(4):
            dwv[rel, lane] = part[lane * 128 : (lane + 1) * 128]

    pl.semaphore_wait(bar, 21)
    for a in (1, 3, 2):
        pp = (p + a) % 4
        remote(
            w_in.at[:, rows(zq, 1024)], wbuf.at[rows(p), rows(zq, 1024)], wx_ss, wx_rs.at[p], dp, block(pp, q)
        )
    spread(g_pieces, q, to_next, to_prev, g_ss, g_rs)
    for b in (1, 3, 2):
        qq = (q + b) % 4
        for f in range(4):
            remote(
                o_in.at[:, rows(block(f, qq))], abuf.at[rows(q), pl.ds(f * 128, 128)], a_ss, a_rs, dp, block(p, qq)
            )
    for a in (1, 3, 2):
        pp = (p + a) % 4
        drain(wbuf.at[rows(pp), rows(zq, 1024)], wx_rs.at[pp])
    spread(w_pieces, zq, to_up, to_down, wz_ss, wz_rs)
    pass_on(g_pieces, g_half, q, to_next, to_prev, g_ss, g_rs)
    send_heads(0)
    for cp in la:
        cp.wait()
    drain(abuf.at[pl.ds(0, 384)], a_rs)
    atbuf[...] = abuf[...].T
    pass_on(w_pieces, w_half, zq, to_up, to_down, wz_ss, wz_rs)
    lg.wait()
    arrive(g_half, g_rs)
    send_heads(1)
    send_heads(2)
    pl.loop(3, 6)(project)
    lw.wait()

    def grad_attn(quarter, begin=False):
        cols = rows(quarter, 1024)
        part = lax.dot_general(gbuf[:, cols], wbuf[:, cols], NT, preferred_element_type=F32)
        gacc[...] = part if begin else gacc[...] + part

    grad_attn(zq, True)
    arrive(w_half, wz_rs, (2, 3))
    grad_attn((zq + 3) % 4)
    grad_attn((zq + 1) % 4)
    arrive(w_half, wz_rs, (4, 5))
    ring_begin()
    grad_attn((zq + 2) % 4)

    for n in range(2):
        for m in range(2):
            f = n * 2 + m
            gf = gacc[:, f * 128 : (f + 1) * 128].astype(BF16)
            gsnd[f] = gf
            prod = gf.astype(F32) * abuf[:, f * 128 : (f + 1) * 128].astype(F32)
            rd = jnp.sum(prod.T, axis=0, keepdims=True)
            for t in range(4):
                rdsnd[f, t] = jnp.broadcast_to(rd[:, t * 128 : (t + 1) * 128], (8, 128))

            @pl.when(p == f)
            def _():
                for b in range(4):
                    pltpu.make_async_copy(gsnd.at[f, pl.ds(b * 128, 128)], gh.at[rows(block(p, b))], ga_loc).start()
                    pltpu.make_async_copy(rdsnd.at[f, b], rdh.at[block(p, b)], rd_loc).start()

            @pl.when(p != f)
            def _():
                for b in range(4):
                    remote(
                        gsnd.at[f, pl.ds(b * 128, 128)], gh.at[rows(block(p, b))], ga_ss, ga_rs, dp, block(f, q)
                    )
                    remote(rdsnd.at[f, b], rdh.at[block(p, b)], rd_ss, rd_rs, dp, block(f, q))

    pl.loop(6, 8)(project)
    pl.loop(0, 3)(project)
    todo = [(0, (0, 2)), (0, (1, 3))]
    todo += [(step, lanes) for step in (1, 2) for lanes in ((2, 0), (3, 1), (0, 2), (1, 3))]
    for _ in range(FIRST_STEPS):
        ring_step(*todo.pop(0))
    dka[...] = jnp.zeros_like(dka)
    dva[...] = jnp.zeros_like(dva)
    for cp in lh:
        cp.wait()
    drain(gsnd.at[0], ga_loc)
    drain(rdsnd.at[0], rd_loc)
    for t, (src, dst) in enumerate(heads):
        drain(dst.at[pl.ds(0, 1920)], h_rs.at[t])
    drain(gsnd.at[pl.ds(0, 3)], ga_rs)
    drain(rdsnd.at[pl.ds(0, 3)], rd_rs)


    def go_on():
        if len(todo) > LAST_STEPS:
            ring_step(*todo.pop(0))

    back = ((dq, oq), (dk, ok), (dv, ov))
    for i in range(NBLK - 1, -1, -1):
        attend(i, first, qh, kh, vh, gh, rdh, dq, sbuf, dka, dva, go_on if i >= 2 else lambda: None)
        qs = pl.ds(i * BLK, BLK)
        dk[qs, :] = (dka[qs, :] * SCALE).astype(BF16)
        dv[qs, :] = dva[qs, :].astype(BF16)
        for t in range(4):
            d = i * 4 + (s + t) % 4

            @pl.when(d == s)
            def _():
                for n, (src, dst) in enumerate(back):
                    pltpu.make_async_copy(src.at[rows(d)], dst.at[:, rows(s)], b_loc.at[n]).start()

            @pl.when(d != s)
            def _():
                for n, (src, dst) in enumerate(back):
                    remote(src.at[rows(d)], dst.at[:, rows(s)], b_ss.at[n], b_rs.at[n], dp, d)
        go_on()
    for step in todo:
        ring_step(*step)

    drain(dwv.at[pl.ds(0, 7)], r_ss)
    for lane in (2, 0, 3, 1):
        drain(slots.at[0, 3, lane], r_rs.at[0, 3, lane])
        drain(slots.at[1, 3, lane], r_rs.at[1, 3, lane])
        dwv[4, lane] = (
            dwv[0, lane].astype(F32) + slots[0, 3, lane].astype(F32) + slots[1, 3, lane].astype(F32)
        ).astype(BF16)
        for cc in range(2):
            piece = dwv.at[4, lane, :, pl.ds(cc * 256, 256)]
            own = (lane == p) & (cc == c)

            @pl.when(own)
            def _():
                pltpu.make_async_copy(piece, tbuf.at[c * 4 + p], t_loc).start()

            @pl.when(jnp.logical_not(own))
            def _():
                remote(piece, tbuf.at[c * 4 + p], t_ss, t_rs, z * 2 + cc, block(lane, q))

    drain(tbuf.at[0], t_loc)
    drain(tbuf.at[pl.ds(0, 7)], t_rs)
    tot = tbuf[0].astype(F32)
    for n in range(1, 8):
        tot += tbuf[n].astype(F32)
    ow[...] = tot

    for n, (src, dst) in enumerate(back):
        drain(src.at[pl.ds(0, 128)], b_loc.at[n])
        drain(src.at[pl.ds(0, 1920)], b_rs.at[n])
        drain(src.at[pl.ds(0, 1920)], b_ss.at[n])
    drain(gbuf.at[pl.ds(0, 384)], g_ss)
    drain(wbuf.at[pl.ds(0, 96)], wx_ss)
    drain(wbuf.at[pl.ds(0, 288)], wz_ss)
    drain(abuf.at[pl.ds(0, 384)], a_ss)
    drain(gsnd.at[pl.ds(0, 3)], ga_ss)
    drain(rdsnd.at[pl.ds(0, 3)], rd_ss)
    drain(tbuf.at[pl.ds(0, 7)], t_ss)
    for t, (src, dst) in enumerate(heads):
        drain(dst.at[pl.ds(0, 1920)], h_ss.at[t])


def run_whole(queries, keys, values, attn, grad_out, w_out, starts):
    any_ = pl.BlockSpec(memory_space=pl.ANY)
    tok = jax.ShapeDtypeStruct((128, 2048), BF16)
    dma = pltpu.SemaphoreType.DMA
    head = pltpu.VMEM((2048, HDIM), BF16)
    acc = pltpu.VMEM((2048, HDIM), F32)
    return pl.pallas_call(
        whole_kernel,
        out_shape=(tok, tok, tok, jax.ShapeDtypeStruct((128, 256), F32)),
        in_specs=[any_] * 6 + [pl.BlockSpec(memory_space=pltpu.SMEM)],
        out_specs=(any_, any_, any_, pl.BlockSpec(memory_space=pltpu.VMEM)),
        scratch_shapes=[
            pltpu.VMEM((512, 4096), BF16), pltpu.VMEM((512, 4096), BF16), pltpu.VMEM((512, 512), F32),
            pltpu.VMEM((512, 512), BF16),
            pltpu.VMEM((512, 512), BF16), pltpu.VMEM((4, 512, 128), BF16), pltpu.VMEM((4, 4, 8, 128), F32),
            pltpu.VMEM((8, 4, 128, 512), BF16), pltpu.VMEM((2, 4, 4, 128, 512), BF16),
            head, head, head, head, pltpu.VMEM((16, 8, 128), F32),
            pltpu.VMEM((2048, BLK), F32), acc, acc, head, head, head,
            pltpu.VMEM((8, 128, 256), BF16),
            dma((6,)), dma((4,)), dma((6,)), dma, dma((3,)), dma, dma, dma((2, 4, 4)), dma((3,)), dma,
            dma, dma, dma, dma, dma((3,)), dma, dma, dma, dma((3,)), dma,
            dma((9,)), dma, dma, dma((3,)), dma,
        ],
        compiler_params=pltpu.CompilerParams(collective_id=0, has_side_effects=True, vmem_limit_bytes=VMEM_LIMIT),
        name="whole",
    )(queries, keys, values, attn, grad_out, w_out, starts)


def finish_kernel(*refs):
    n = len(refs) // 2
    for i in range(n):
        refs[n + i][...] = refs[i][...]


def finish(*arrays):
    vm = pl.BlockSpec(memory_space=pltpu.VMEM)
    return pl.pallas_call(
        finish_kernel,
        out_shape=tuple(jax.ShapeDtypeStruct(a.shape, a.dtype) for a in arrays),
        in_specs=[vm] * len(arrays),
        out_specs=(vm,) * len(arrays),
        name="finish",
    )(*arrays)


def shards(queries, keys, values, attn, grad_out, w_out, starts):
    return finish(*run_whole(queries, keys, values, attn, grad_out, w_out, starts))


def solution(mesh):
    tok = P(("dp", "seq"), None)
    return jax.shard_map(
        shards,
        mesh=mesh,
        in_specs=(tok, tok, tok, tok, tok, P("seq", None), P("dp", None)),
        out_specs=(tok, tok, tok, P("seq", "dp")),
        check_vma=False,
    )
```

```python
import functools

import jax
import jax.numpy as jnp
from jax import lax
from jax.experimental import pallas as pl
from jax.experimental.pallas import tpu as pltpu
from jax.sharding import PartitionSpec as P

HDIM = 128
MESH = pl.DeviceIdType.MESH
BF16 = jnp.bfloat16
F32 = jnp.float32
NT = (((1,), (1,)), ((), ()))
NN = (((1,), (0,)), ((), ()))
TN = (((0,), (0,)), ((), ()))
VMEM_LIMIT = 56 << 20


def place():
    dp = lax.axis_index("dp")
    s = lax.axis_index("seq")
    c = dp % 2
    x, y = s // 4, s % 4
    p = x * (1 - c) + y * c
    q = y * (1 - c) + x * c
    sp, sq = 4 - 3 * c, 1 + 3 * c

    def block(pp, qq):
        return pp * sp + qq * sq

    return dp, c, s, p, q, block


def remote(src, dst, ssem, rsem, dp, s):
    cp = pltpu.make_async_remote_copy(
        src_ref=src, dst_ref=dst, send_sem=ssem, recv_sem=rsem, device_id=(dp, s), device_id_type=MESH
    )
    cp.start()


def drain(ref, sem):
    pltpu.make_async_copy(ref, ref, sem).wait()


def rows(i, n=128):
    return pl.ds(pl.multiple_of(i * n, n), n)


BLK = 512
NBLK = 2048 // BLK
SCALE = HDIM ** (-0.5)
LOG2E = 1.4426950408889634
FIRST_STEPS = 1
LAST_STEPS = 2


def spread(pieces, me, send_next, send_prev, ss, rs):
    for half, send, sem in ((0, send_next, 0), (1, send_prev, 1), (1, send_next, 2), (0, send_prev, 3)):
        for src, dst in pieces(me, half):
            send(src, dst, ss, rs.at[sem])


def pass_on(pieces, relayed, whole, me, send_next, send_prev, ss, rs):
    nxt, prv = (me + 1) % 4, (me + 3) % 4
    drain(whole, rs.at[0])
    for _, ref in relayed(prv, 0):
        send_next(ref, ref, ss, rs.at[4])
    drain(whole, rs.at[1])
    for _, ref in relayed(nxt, 1):
        send_prev(ref, ref, ss, rs.at[5])


def arrive(whole, rs, sems=(2, 3, 4, 5)):
    for sem in sems:
        drain(whole, rs.at[sem])


def pair(i, j):
    return pl.ds((i * (i + 1) // 2 + j) * BLK, BLK)


def weigh(i, first, q, k, sbuf):
    qs = pl.ds(i * BLK, BLK)
    pos = lax.broadcasted_iota(jnp.int32, (1, BLK), 1) + i * BLK
    seg = jnp.zeros((1, BLK), jnp.int32)
    for e in range(8):
        st = first[0, e]
        seg = jnp.where(pos >= st, jnp.maximum(seg, st), seg)
    kp = lax.broadcasted_iota(jnp.int32, (BLK, BLK), 0)
    m = jnp.full((8, BLK), -1e30, F32)
    for j in range(i + 1):
        sc = lax.dot_general(
            k[pl.ds(j * BLK, BLK), :], q[qs, :], NT, preferred_element_type=F32
        ) * (SCALE * LOG2E)
        live = kp >= seg - j * BLK
        if j == i:
            live = live & (kp <= pos - j * BLK)
        sc = jnp.where(live, sc, -1e30)
        sbuf[pair(i, j), :] = sc
        m = jnp.maximum(m, jnp.max(sc.reshape(BLK // 8, 8, BLK), axis=0))
    m = jnp.max(m, axis=0, keepdims=True)
    tot = jnp.zeros((8, BLK), F32)
    for j in range(i + 1):
        e = jnp.exp2(sbuf[pair(i, j), :] - m)
        sbuf[pair(i, j), :] = e
        tot = tot + jnp.sum(e.reshape(BLK // 8, 8, BLK), axis=0)
    return 1.0 / jnp.sum(tot, axis=0, keepdims=True)


def attend(i, inv, q, k, v, g, rd, dq, sbuf, dka, dva):
    qs = pl.ds(i * BLK, BLK)
    rdi = jnp.concatenate([rd[i * (BLK // 128) + t][:1] for t in range(BLK // 128)], axis=1)
    acc = jnp.zeros((BLK, HDIM), F32)
    for j in range(i + 1):
        ks = pl.ds(j * BLK, BLK)
        prob = sbuf[pair(i, j), :] * inv
        gp = lax.dot_general(v[ks, :], g[qs, :], NT, preferred_element_type=F32)
        ds = (prob * (gp - rdi)).astype(BF16)
        dva[ks, :] += lax.dot_general(prob.astype(BF16), g[qs, :], NN, preferred_element_type=F32)
        dka[ks, :] += lax.dot_general(ds, q[qs, :], NN, preferred_element_type=F32)
        acc = acc + lax.dot_general(ds, k[ks, :], TN, preferred_element_type=F32)
    dq[qs, :] = (acc * SCALE).astype(BF16)


def whole_kernel(
    q_in, k_in, v_in, o_in, g_in, w_in, first,
    oq, ok, ov, ow,
    gbuf, wbuf, gacc, abuf, atbuf, gsnd, rdsnd, dwv, slots, qh, kh, vh, gh, rdh,
    sbuf, dka, dva, dq, dk, dv, tbuf,
    g_rs, wx_rs, wy_rs, wz_rs, a_rs, h_rs, ga_rs, rd_rs, r_rs, b_rs, t_rs,
    g_ss, wx_ss, wz_ss, a_ss, h_ss, ga_ss, rd_ss, r_ss, b_ss, t_ss,
    loc, ga_loc, rd_loc, b_loc, t_loc,
):
    dp, c, s, p, q, block = place()
    z = dp // 2
    zq = z % 4
    up, down = ((z + 1) % 8) * 2 + c, ((z + 7) % 8) * 2 + c
    mate = z * 2 + 1 - c
    bar = pltpu.get_barrier_semaphore()
    for a in range(4):
        for b in range(4):
            if a or b:
                pl.semaphore_signal(
                    bar, 1, device_id=(dp, block((p + a) % 4, (q + b) % 4)), device_id_type=MESH
                )
    for d in (up, down, mate):
        pl.semaphore_signal(bar, 1, device_id=(d, s), device_id_type=MESH)
    for a in range(1, 4):
        pl.semaphore_signal(bar, 1, device_id=(mate, block(p, (q + a) % 4)), device_id_type=MESH)

    lg = pltpu.make_async_copy(g_in, gbuf.at[rows(q)], loc.at[0])
    lw = pltpu.make_async_copy(w_in, wbuf.at[rows(p)], loc.at[1])
    lg.start()
    lw.start()
    la = []
    for pp in range(4):
        cp = pltpu.make_async_copy(
            o_in.at[:, rows(block(pp, q))], abuf.at[rows(q), pl.ds(pp * 128, 128)], loc.at[2 + pp]
        )
        cp.start()
        la.append(cp)
    heads = ((q_in, qh), (k_in, kh), (v_in, vh))
    lh = []
    for t, (src, dst) in enumerate(heads):
        cp = pltpu.make_async_copy(src.at[:, rows(s)], dst.at[rows(s)], loc.at[6 + t])
        cp.start()
        lh.append(cp)

    def to_next(src, dst, ssem, rsem):
        remote(src, dst, ssem, rsem, dp, block(p, (q + 1) % 4))

    def to_prev(src, dst, ssem, rsem):
        remote(src, dst, ssem, rsem, dp, block(p, (q + 3) % 4))

    def to_up(src, dst, ssem, rsem):
        remote(src, dst, ssem, rsem, up, s)

    def to_down(src, dst, ssem, rsem):
        remote(src, dst, ssem, rsem, down, s)

    def g_pieces(who, half):
        ref = gbuf.at[rows(who * 2 + half, 64)]
        return [(g_in.at[pl.ds(half * 64, 64)], ref)]

    def w_pieces(who, half):
        refs = [wbuf.at[rows(((p + a) % 4) * 2 + half, 64), rows(who, 1024)] for a in range(1, 4)]
        return [(ref, ref) for ref in refs]

    def w_relayed(who, half):
        refs = [wbuf.at[rows(((p + a) % 4) * 2 + half, 64), rows(who * 2 + 1, 512)] for a in range(1, 4)]
        return [(ref, ref) for ref in refs]

    g_half, w_half = gbuf.at[pl.ds(0, 64)], wbuf.at[pl.ds(0, 192), pl.ds(0, 1024)]

    def send_heads(t):
        src, dst = heads[t]
        for a in range(4):
            for b in range(4):
                if a or b:
                    d = block((p + a) % 4, (q + b) % 4)
                    remote(src.at[:, rows(d)], dst.at[rows(s)], h_ss.at[t], h_rs.at[t], dp, d)

    def ring_put(way, step, lane, src):
        remote(src, slots.at[way, step, lane], r_ss, r_rs.at[way, step, lane], (up, down)[way], s)

    def ring_begin():
        for lane in range(2):
            ring_put(0, 0, lane, dwv.at[4, lane])
            ring_put(1, 0, lane + 2, dwv.at[4, lane + 2])
        for lane in range(2):
            ring_put(0, 1, lane + 2, dwv.at[3, lane + 2])
            ring_put(1, 1, lane, dwv.at[5, lane])

    def ring_step(step, lanes):
        for way, lane in enumerate(lanes):
            got = slots.at[way, step, lane]
            drain(got, r_rs.at[way, step, lane])
            ahead = (3 - step, 5 + step)[way]
            slots[way, step, lane] = (got[...].astype(F32) + dwv[ahead, lane].astype(F32)).astype(BF16)
            ring_put(way, step + 1, lane, got)

    def project(rel):
        part = lax.dot_general(
            atbuf[...], gbuf[:, rows((z + rel) % 8, 512)], NN, preferred_element_type=F32
        ).astype(BF16)
        for lane in range(4):
            dwv[rel, lane] = part[lane * 128 : (lane + 1) * 128]

    pl.semaphore_wait(bar, 21)
    for a in (1, 3, 2):
        pp = (p + a) % 4
        remote(
            w_in.at[:, rows(zq, 1024)], wbuf.at[rows(p), rows(zq, 1024)], wx_ss, wx_rs.at[p], dp, block(pp, q)
        )
    spread(g_pieces, q, to_next, to_prev, g_ss, g_rs)
    far = (zq + 2) % 4 * 2
    for a in (1, 3, 2):
        pp = (p + a) % 4
        remote(
            w_in.at[:, rows(far, 512)], wbuf.at[rows(p), rows(far, 512)], wx_ss, wy_rs.at[p], dp, block(pp, q)
        )
    for b in (1, 3, 2):
        qq = (q + b) % 4
        for f in range(4):
            remote(
                o_in.at[:, rows(block(f, qq))], abuf.at[rows(q), pl.ds(f * 128, 128)], a_ss, a_rs, dp, block(p, qq)
            )
    for a in (1, 3, 2):
        pp = (p + a) % 4
        drain(wbuf.at[rows(pp), rows(zq, 1024)], wx_rs.at[pp])
    spread(w_pieces, zq, to_up, to_down, wz_ss, wz_rs)
    pass_on(g_pieces, g_pieces, g_half, q, to_next, to_prev, g_ss, g_rs)
    send_heads(0)
    for cp in la:
        cp.wait()
    drain(abuf.at[pl.ds(0, 384)], a_rs)
    atbuf[...] = abuf[...].T
    pass_on(w_pieces, w_relayed, w_half, zq, to_up, to_down, wz_ss, wz_rs)
    lg.wait()
    arrive(g_half, g_rs)
    send_heads(1)
    send_heads(2)
    pl.loop(3, 6)(project)
    lw.wait()

    def grad_attn(quarter, begin=False):
        cols = rows(quarter, 1024)
        part = lax.dot_general(gbuf[:, cols], wbuf[:, cols], NT, preferred_element_type=F32)
        gacc[...] = part if begin else gacc[...] + part

    grad_attn(zq, True)
    arrive(w_half, wz_rs, (2, 3))
    grad_attn((zq + 3) % 4)
    grad_attn((zq + 1) % 4)
    arrive(wbuf.at[pl.ds(0, 192), pl.ds(0, 512)], wz_rs, (4, 5))
    for a in (1, 3, 2):
        pp = (p + a) % 4
        drain(wbuf.at[rows(pp), rows(far, 512)], wy_rs.at[pp])
    ring_begin()
    grad_attn((zq + 2) % 4)

    for n in range(2):
        for m in range(2):
            f = n * 2 + m
            gf = gacc[:, f * 128 : (f + 1) * 128].astype(BF16)
            gsnd[f] = gf
            prod = gf.astype(F32) * abuf[:, f * 128 : (f + 1) * 128].astype(F32)
            rd = jnp.sum(prod.T, axis=0, keepdims=True)
            for t in range(4):
                rdsnd[f, t] = jnp.broadcast_to(rd[:, t * 128 : (t + 1) * 128], (8, 128))

            @pl.when(p == f)
            def _():
                for b in range(4):
                    pltpu.make_async_copy(gsnd.at[f, pl.ds(b * 128, 128)], gh.at[rows(block(p, b))], ga_loc).start()
                    pltpu.make_async_copy(rdsnd.at[f, b], rdh.at[block(p, b)], rd_loc).start()

            @pl.when(p != f)
            def _():
                for b in range(4):
                    remote(
                        gsnd.at[f, pl.ds(b * 128, 128)], gh.at[rows(block(p, b))], ga_ss, ga_rs, dp, block(f, q)
                    )
                    remote(rdsnd.at[f, b], rdh.at[block(p, b)], rd_ss, rd_rs, dp, block(f, q))

    pl.loop(6, 8)(project)
    pl.loop(0, 3)(project)
    todo = [(0, (0, 2)), (0, (1, 3))]
    todo += [(step, lanes) for step in (1, 2) for lanes in ((2, 0), (3, 1), (0, 2), (1, 3))]
    for _ in range(FIRST_STEPS):
        ring_step(*todo.pop(0))
    dka[...] = jnp.zeros_like(dka)
    dva[...] = jnp.zeros_like(dva)
    for cp in lh:
        cp.wait()

    def go_on():
        if len(todo) > LAST_STEPS:
            ring_step(*todo.pop(0))

    drain(qh.at[pl.ds(0, 1920)], h_rs.at[0])
    drain(kh.at[pl.ds(0, 1920)], h_rs.at[1])
    inv = [None] * NBLK
    for i in range(NBLK - 1, -1, -1):
        inv[i] = weigh(i, first, qh, kh, sbuf)
        if i >= 2:
            go_on()
    drain(vh.at[pl.ds(0, 1920)], h_rs.at[2])
    drain(gsnd.at[0], ga_loc)
    drain(rdsnd.at[0], rd_loc)
    drain(gsnd.at[pl.ds(0, 3)], ga_rs)
    drain(rdsnd.at[pl.ds(0, 3)], rd_rs)

    back = ((dq, oq), (dk, ok), (dv, ov))
    for i in range(NBLK - 1, -1, -1):
        attend(i, inv[i], qh, kh, vh, gh, rdh, dq, sbuf, dka, dva)
        qs = pl.ds(i * BLK, BLK)
        dk[qs, :] = (dka[qs, :] * SCALE).astype(BF16)
        dv[qs, :] = dva[qs, :].astype(BF16)
        for t in range(4):
            d = i * 4 + (s + t) % 4

            @pl.when(d == s)
            def _():
                for n, (src, dst) in enumerate(back):
                    pltpu.make_async_copy(src.at[rows(d)], dst.at[:, rows(s)], b_loc.at[n]).start()

            @pl.when(d != s)
            def _():
                for n, (src, dst) in enumerate(back):
                    remote(src.at[rows(d)], dst.at[:, rows(s)], b_ss.at[n], b_rs.at[n], dp, d)
        go_on()
    for step in todo:
        ring_step(*step)

    drain(dwv.at[pl.ds(0, 7)], r_ss)
    for lane in (2, 0, 3, 1):
        drain(slots.at[0, 3, lane], r_rs.at[0, 3, lane])
        drain(slots.at[1, 3, lane], r_rs.at[1, 3, lane])
        dwv[4, lane] = (
            dwv[0, lane].astype(F32) + slots[0, 3, lane].astype(F32) + slots[1, 3, lane].astype(F32)
        ).astype(BF16)
        for cc in range(2):
            piece = dwv.at[4, lane, :, pl.ds(cc * 256, 256)]
            own = (lane == p) & (cc == c)

            @pl.when(own)
            def _():
                pltpu.make_async_copy(piece, tbuf.at[c * 4 + p], t_loc).start()

            @pl.when(jnp.logical_not(own))
            def _():
                remote(piece, tbuf.at[c * 4 + p], t_ss, t_rs, z * 2 + cc, block(lane, q))

    drain(tbuf.at[0], t_loc)
    drain(tbuf.at[pl.ds(0, 7)], t_rs)
    tot = tbuf[0].astype(F32)
    for n in range(1, 8):
        tot += tbuf[n].astype(F32)
    ow[...] = tot

    for n, (src, dst) in enumerate(back):
        drain(src.at[pl.ds(0, 128)], b_loc.at[n])
        drain(src.at[pl.ds(0, 1920)], b_rs.at[n])
        drain(src.at[pl.ds(0, 1920)], b_ss.at[n])
    drain(gbuf.at[pl.ds(0, 384)], g_ss)
    drain(wbuf.at[pl.ds(0, 144)], wx_ss)
    drain(wbuf.at[pl.ds(0, 240)], wz_ss)
    drain(abuf.at[pl.ds(0, 384)], a_ss)
    drain(gsnd.at[pl.ds(0, 3)], ga_ss)
    drain(rdsnd.at[pl.ds(0, 3)], rd_ss)
    drain(tbuf.at[pl.ds(0, 7)], t_ss)
    for t, (src, dst) in enumerate(heads):
        drain(dst.at[pl.ds(0, 1920)], h_ss.at[t])


def run_whole(queries, keys, values, attn, grad_out, w_out, starts):
    any_ = pl.BlockSpec(memory_space=pl.ANY)
    tok = jax.ShapeDtypeStruct((128, 2048), BF16)
    dma = pltpu.SemaphoreType.DMA
    head = pltpu.VMEM((2048, HDIM), BF16)
    acc = pltpu.VMEM((2048, HDIM), F32)
    return pl.pallas_call(
        whole_kernel,
        out_shape=(tok, tok, tok, jax.ShapeDtypeStruct((128, 256), F32)),
        in_specs=[any_] * 6 + [pl.BlockSpec(memory_space=pltpu.SMEM)],
        out_specs=(any_, any_, any_, pl.BlockSpec(memory_space=pltpu.VMEM)),
        scratch_shapes=[
            pltpu.VMEM((512, 4096), BF16), pltpu.VMEM((512, 4096), BF16), pltpu.VMEM((512, 512), F32),
            pltpu.VMEM((512, 512), BF16),
            pltpu.VMEM((512, 512), BF16), pltpu.VMEM((4, 512, 128), BF16), pltpu.VMEM((4, 4, 8, 128), F32),
            pltpu.VMEM((8, 4, 128, 512), BF16), pltpu.VMEM((2, 4, 4, 128, 512), BF16),
            head, head, head, head, pltpu.VMEM((16, 8, 128), F32),
            pltpu.VMEM((NBLK * (NBLK + 1) // 2 * BLK, BLK), F32), acc, acc, head, head, head,
            pltpu.VMEM((8, 128, 256), BF16),
            dma((6,)), dma((4,)), dma((4,)), dma((6,)), dma, dma((3,)), dma, dma, dma((2, 4, 4)), dma((3,)), dma,
            dma, dma, dma, dma, dma((3,)), dma, dma, dma, dma((3,)), dma,
            dma((9,)), dma, dma, dma((3,)), dma,
        ],
        compiler_params=pltpu.CompilerParams(collective_id=0, has_side_effects=True, vmem_limit_bytes=VMEM_LIMIT),
        name="whole",
    )(queries, keys, values, attn, grad_out, w_out, starts)


def finish_kernel(*refs):
    n = len(refs) // 2
    for i in range(n):
        refs[n + i][...] = refs[i][...]


def finish(*arrays):
    vm = pl.BlockSpec(memory_space=pltpu.VMEM)
    return pl.pallas_call(
        finish_kernel,
        out_shape=tuple(jax.ShapeDtypeStruct(a.shape, a.dtype) for a in arrays),
        in_specs=[vm] * len(arrays),
        out_specs=(vm,) * len(arrays),
        name="finish",
    )(*arrays)


def shards(queries, keys, values, attn, grad_out, w_out, starts):
    return finish(*run_whole(queries, keys, values, attn, grad_out, w_out, starts))


def solution(mesh):
    tok = P(("dp", "seq"), None)
    return jax.shard_map(
        shards,
        mesh=mesh,
        in_specs=(tok, tok, tok, tok, tok, P("seq", None), P("dp", None)),
        out_specs=(tok, tok, tok, P("seq", "dp")),
        check_vma=False,
    )
```
